32 devices in a mesh: groups: 2 (over x), dev: 8 (over z, y), side: 2 (over core).
Axes of the slice: x: 2, y: 2, z: 4, core: 2. Of those that a mesh axis runs over, the one named last changes fastest.
Arguments:
- states: float32 [64, 16, 128, 128], P(('groups', 'dev', 'side')), parts along dimension 0, may hold values from -6 to 6
- swap_pairs: int32 [4, 2], P('groups'), parts along dimension 0, may hold values from 0 to 31, as said below
- token_counts: int32 [64], P(('groups', 'dev', 'side')), parts along dimension 0, may hold values from 1 to 16, 256 in all
- query_vectors: bfloat16 [64, 16, 2048], P(('groups', 'dev', 'side')), parts along dimension 0, may hold values from -6 to 6
- key_vectors: bfloat16 [64, 16, 2048], P(('groups', 'dev', 'side')), parts along dimension 0, may hold values from -6 to 6
- value_vectors: bfloat16 [64, 16, 2048], P(('groups', 'dev', 'side')), parts along dimension 0, may hold values from -6 to 6
- decay_log: float32 [64, 16, 2048], P(('groups', 'dev', 'side')), parts along dimension 0, may hold values from 0.003 to 0.4
- write_rate: float32 [64, 16, 16], P(('groups', 'dev', 'side')), parts along dimension 0, may hold values from 0.1 to 1
- hidden_rows: bfloat16 [64, 16, 2304], P(('groups', 'dev', 'side')), parts along dimension 0, may hold values from -6 to 6
- expert_ids: int32 [64, 16, 8], P(('groups', 'dev', 'side')), parts along dimension 0, may hold values from 0 to 15, all different within a row; in each aligned block of 16 rows (0 to 15, 16 to 31, ..., all dimensions but the last counted through in order) at most 16 rows name the same one
- route_weights: float32 [64, 16, 8], P(('groups', 'dev', 'side')), parts along dimension 0, may hold values from 0.05 to 0.3
- gate_up_weight: bfloat16 [16, 2304, 1024], P(('dev', 'side')), may hold values from -0.125 to 0.125
- down_weight: bfloat16 [16, 512, 2304], P(('dev', 'side')), may hold values from -0.25 to 0.25
Outputs:
- new_states: float32 [64, 16, 128, 128], P(('groups', 'dev', 'side')), parts along dimension 0
- attention_out: bfloat16 [64, 16, 2048], P(('groups', 'dev', 'side')), parts along dimension 0
- expert_out: bfloat16 [64, 16, 2304], P(('groups', 'dev', 'side')), parts along dimension 0
The draws below stay inside these ranges and needn't reach their ends.
There are 2 independent parts, one for each index of `groups`. The reference program is written for one: setup_inputs(seed, part) draws one part's arguments, and reference() takes and returns one part's arrays. A program takes and returns all parts, laid end to end along the dimension named above; an argument that names none is the same for every part. Nothing has to cross between parts.
Inputs may be any that keep to these rules, and one draw needn't show every extreme that they name: `swap_pairs`: the 4 entries are distinct request slots; slots 0 and 31 are always among them. `token_counts`: the counts of all 32 slots sum to 256, and some slot has exactly 16. `expert_ids`: A token names 8 different experts. In each aligned block of 16 rows (tokens in slot order), no expert is named by more than 16 rows, a bound that some block reaches.
All inputs are finite; a program needn't handle non-finite values. No bound on the sum of `token_counts` on one device may be relied on, other than what follows from the above.
Results may differ from the reference program's by a relative error of at most 0.006.
Values may be sent and summed in bfloat16 or wider, within the bound.
No kernel may reach another device: no remote copies, remote signals or barrier semaphores. Data moves between devices by JAX's collectives and lax.ppermute only.
A program may use at most 64 MiB of HBM per device.

```python
import math
import jax
import jax.numpy as jnp
import numpy as np
from jax import lax

D = 2304
FF = 512
H = 16
DK = 128
DV = 128
TOP = 8
T_MAX = 16
MICRO = 2
MIG = 2
REQ_DEV = 2
EXPERTS = 16
REQS = 32
CAP = 16


def draw_swap_pairs(key, part):
    key = jax.random.fold_in(key, 7)
    inner_key = jax.random.fold_in(key, 1)
    order_key = jax.random.fold_in(key, 2)
    middle = jax.random.permutation(inner_key, REQS - 2).astype(jnp.int32) + 1
    ends = jnp.array([REQS - 1, 0], dtype=jnp.int32)
    entries = jnp.concatenate([ends, middle[:2 * MIG - 2]])
    placing = jax.random.permutation(order_key, 2 * MIG)
    return entries[placing].reshape(MIG, 2).astype(jnp.int32)


def level_of(own_key, shape, split, smallest, top_value):
    loudness = 1.0
    for axis_at, blocks in split:
        heights = jax.random.uniform(jax.random.fold_in(jax.random.fold_in(own_key, 6), axis_at), (blocks,), jnp.float32, smallest / len(split), top_value / len(split))
        loudness = loudness * jnp.repeat(jnp.exp(heights), shape[axis_at] // blocks).reshape((-1,) + (1,) * (len(shape) - 1 - axis_at))
    return loudness


def split_up(amount, total, reach, slope):
    weights = [(1 << 20) // math.isqrt(rank ** slope) + 1 for rank in range(2, amount + 1)]
    surplus, holding = total - reach - (amount - 1), [1] * (amount - 1)
    while surplus > 0:
        free = [i for i in range(amount - 1) if holding[i] < reach]
        mass, remaining = sum([weights[i] for i in free]), surplus
        for i in free:
            extra = min(reach - holding[i], max(1, remaining * weights[i] // mass), surplus)
            holding[i] = holding[i] + extra
            surplus = surplus - extra
    return np.array([reach] + holding)


def ragged_sizes(key, amount, total, most, skew):
    if amount == 2:
        one = jax.random.randint(key, (), max(1, total - most), min(most, total - 1) + 1)
        return jnp.stack([one, total - one])
    tallies = jnp.asarray(split_up(amount, total, most, skew), jnp.int32)
    twos = (amount - 1) // 2
    giver, taker = tallies[1:1 + 2 * twos:2], tallies[2:2 + 2 * twos:2]
    slack = jnp.minimum(giver - 1, most - taker)
    shifted = jax.random.randint(jax.random.fold_in(key, 1), (twos,), 0, 1 << 20) % (slack + 1)
    tallies = tallies.at[1:1 + 2 * twos:2].set(giver - shifted).at[2:2 + 2 * twos:2].set(taker + shifted)
    return tallies[jax.random.permutation(jax.random.fold_in(key, 2), amount)]


def routed_block(rng, own, number, rows, number_of, top, most, skew):
    order = jax.random.permutation(rng, number_of)
    packed, common = load_shares(number_of, rows * top, most, skew, True), load_shares(number_of, rows * top, most, skew, False)
    places = jnp.arange(number_of)

    def named(tallies, rotation):
        used = int((tallies > 0).sum())
        fixed = max(1, used // 4)
        passed = fixed + (places - fixed + rotation * (used - fixed)) % max(1, number_of - fixed)
        return jnp.zeros((number_of,), jnp.int32).at[order[jnp.where(places < fixed, places, passed)]].set(jnp.asarray(tallies, jnp.int32))

    tallies = jnp.where(number % 4 == 0, named(packed, number // 4), named(common, number - number // 4 - 1))
    mixed = jax.random.permutation(jax.random.fold_in(own, 3), number_of)
    source_of, sink = mixed[0:number_of // 2 * 2:2], mixed[1:number_of // 2 * 2:2]
    margin = jnp.minimum(tallies[source_of] - 1, most - tallies[sink]) // 2
    margin = jnp.where((source_of == order[0]) | (sink == order[0]) | (tallies[sink] == 0), 0, jnp.maximum(margin, 0))
    passed = jax.random.randint(jax.random.fold_in(own, 4), (number_of // 2,), 0, 1 << 20) % (margin + 1)
    tallies = tallies.at[source_of].add(-passed).at[sink].add(passed)
    members = jnp.searchsorted(jnp.cumsum(tallies), jnp.arange(rows * top), side="right").astype(jnp.int32)
    table = members.reshape(top, rows).T
    table = table[jax.random.permutation(jax.random.fold_in(own, 1), rows)]
    rotation = jax.random.randint(jax.random.fold_in(own, 2), (rows, 1), 0, top)
    return jnp.take_along_axis(table, (jnp.arange(top)[None, :] + rotation) % top, axis=1)


def load_shares(amount, total, most, lean, full):
    portions = [(1 << 20) // math.isqrt(standing ** lean) + 1 for standing in range(1, amount + 1)]
    largest = most if full else min(most, max(-(-total // amount), total * portions[0] // sum(portions)))
    least = 1 if total - largest >= amount - 1 else 0
    counts, spare = [largest] + [least] * (amount - 1), total - largest - least * (amount - 1)
    while spare > 0:
        free = [i for i in range(1, amount) if counts[i] < largest] or [i for i in range(1, amount) if counts[i] < most]
        pool, budget = sum([portions[i] for i in free]), spare
        for i in free:
            more = min(most - counts[i], max(1, budget * portions[i] // pool), spare)
            counts[i] = counts[i] + more
            spare = spare - more
    return np.array(counts)


def scatter_about(stream_key, extent, spread, reach, pieces=(), kind=jnp.bfloat16):
    loudness = level_of(stream_key, extent, pieces, -0.22, 0.18) if pieces else 1.0
    values = jax.random.normal(stream_key, extent, jnp.float32) * spread * loudness
    return jnp.minimum(jnp.maximum(values, -reach), reach).astype(kind)


def setup_inputs(seed: int = 0, part: int = 0) -> dict:
    key_of = jax.random.split(jax.random.key(seed), 14)
    part_splits = jax.random.split(jax.random.fold_in(key_of[13], part), 14)
    states = scatter_about(part_splits[0], (REQS, H, DK, DV), 1.0, 6.0, ((0, 16),), jnp.float32)
    swap_pairs = draw_swap_pairs(jax.random.fold_in(jax.random.fold_in(key_of[13], part), 71), part)
    token_counts = ragged_sizes(part_splits[2], REQS, REQS * T_MAX // 2, T_MAX, 1).astype(jnp.int32)
    query_vectors = scatter_about(part_splits[3], (REQS, T_MAX, H * DK), 1.0, 6.0, ((0, 16),))
    key_vectors = scatter_about(part_splits[4], (REQS, T_MAX, H * DK), 1.0, 6.0, ((0, 16),))
    value_vectors = scatter_about(part_splits[5], (REQS, T_MAX, H * DV), 1.0, 6.0, ((0, 16),))
    decay_log = jnp.clip(jnp.exp(math.log(0.4) - 4.8928523 * jax.random.uniform(part_splits[6], (REQS, T_MAX, H * DK), jnp.float32) ** level_of(part_splits[6], (REQS, T_MAX, H * DK), ((0, 16),), -0.2, 0.2)), 0.003, 0.4)
    write_rate = jnp.clip(0.1 + 0.9 * jax.random.uniform(part_splits[7], (REQS, T_MAX, H), jnp.float32) ** level_of(part_splits[7], (REQS, T_MAX, H), ((0, 16),), -0.2, 0.2), 0.1, 1.0)
    hidden_rows = scatter_about(part_splits[8], (REQS, T_MAX, D), 1.0, 6.0, ((0, 16),))
    expert_ids_keys = jax.random.split(jax.random.fold_in(part_splits[9], 1), REQS * T_MAX // (REQ_DEV * T_MAX // MICRO))
    expert_ids_turns = jax.random.permutation(jax.random.fold_in(part_splits[9], 3), REQS * T_MAX // (REQ_DEV * T_MAX // MICRO))
    expert_ids = jax.vmap(lambda own, number: routed_block(jax.random.fold_in(part_splits[9], 2), own, number, REQ_DEV * T_MAX // MICRO, EXPERTS, TOP, CAP, 2))(expert_ids_keys, expert_ids_turns).reshape((REQS, T_MAX, TOP))
    route_weights = jnp.clip(0.05 + 0.25 * jax.random.uniform(part_splits[10], (REQS, T_MAX, TOP), jnp.float32) ** level_of(part_splits[10], (REQS, T_MAX, TOP), ((0, 16),), -0.2, 0.2), 0.05, 0.3)
    gate_up_weight = scatter_about(key_of[11], (EXPERTS, D, 2 * FF), D ** -0.5, 0.125, ((0, 16),))
    down_weight = scatter_about(key_of[12], (EXPERTS, FF, D), FF ** -0.5, 0.25, ((0, 16),))
    return dict(states=states, swap_pairs=swap_pairs, token_counts=token_counts, query_vectors=query_vectors, key_vectors=key_vectors, value_vectors=value_vectors, decay_log=decay_log, write_rate=write_rate, hidden_rows=hidden_rows, expert_ids=expert_ids, route_weights=route_weights, gate_up_weight=gate_up_weight, down_weight=down_weight)


def normalize(vectors):
    widened = vectors.astype(jnp.float32).reshape(REQS, T_MAX, H, DK)
    return widened / jnp.sqrt(lax.optimization_barrier(jnp.sum(widened * widened, axis=-1, keepdims=True)) + 1e-06)

def advance(carried, inputs):
    query_now, key_now, value_now, retention_now, rate_now, active = inputs
    decayed = carried * retention_now[..., None]
    predicted = jnp.einsum('rhkv,rhk->rhv', decayed, key_now, precision=lax.Precision.HIGHEST)
    updated = decayed + rate_now[..., None, None] * key_now[..., None] * (value_now - predicted)[:, :, None, :]
    output = jnp.einsum('rhkv,rhk->rhv', updated, query_now, precision=lax.Precision.HIGHEST)
    carried = jnp.where(active[:, None, None, None], updated, carried)
    output = jnp.where(active[:, None, None], output, jnp.zeros_like(output))
    return (carried, output)

def reference(states, swap_pairs, token_counts, query_vectors, key_vectors, value_vectors, decay_log, write_rate, hidden_rows, expert_ids, route_weights, gate_up_weight, down_weight):
    slot_order = jnp.arange(REQS, dtype=jnp.int32)
    first_slot = swap_pairs[:, 0]
    second = swap_pairs[:, 1]
    source = slot_order.at[first_slot].set(second).at[second].set(first_slot)
    migrated = states[source]
    queries = normalize(query_vectors)
    unit_keys = normalize(key_vectors)
    value_rows = value_vectors.astype(jnp.float32).reshape(REQS, T_MAX, H, DV)
    retention = jnp.exp(-decay_log).reshape(REQS, T_MAX, H, DK)
    times_now = jnp.arange(T_MAX, dtype=jnp.int32)
    active = times_now[:, None] < token_counts[None, :]
    inputs = (jnp.moveaxis(queries, 1, 0), jnp.moveaxis(unit_keys, 1, 0), jnp.moveaxis(value_rows, 1, 0), jnp.moveaxis(retention, 1, 0), jnp.moveaxis(write_rate, 1, 0), active)
    final_states, outputs = lax.scan(advance, migrated, inputs)
    attention_out = jnp.moveaxis(outputs, 0, 1).reshape(REQS, T_MAX, H * DV).astype(jnp.bfloat16)
    rows_flat = hidden_rows.reshape(REQS * T_MAX, D)
    flat_ids = expert_ids.reshape(-1)
    flat_weights = route_weights.reshape(-1)
    limit = min(REQS * T_MAX, MICRO * CAP * EXPERTS)

    def per_expert(accumulated, expert):
        matches = flat_ids == expert
        chosen = jnp.nonzero(matches, size=limit, fill_value=0)[0].astype(jnp.int32)
        is_valid = jnp.arange(limit, dtype=jnp.int32) < jnp.sum(matches.astype(jnp.int32))
        picked_rows = rows_flat[chosen // TOP]
        gate_up = jnp.dot(picked_rows, gate_up_weight[expert], preferred_element_type=jnp.float32)
        activated = (jax.nn.silu(gate_up[:, :FF]) * gate_up[:, FF:]).astype(jnp.bfloat16)
        produced = jnp.dot(activated, down_weight[expert], preferred_element_type=jnp.float32).astype(jnp.bfloat16)
        scaling = jnp.where(is_valid, flat_weights[chosen], jnp.zeros_like(flat_weights[chosen]))
        weighted = produced.astype(jnp.float32) * scaling[:, None]
        return (accumulated.at[chosen // TOP].add(weighted), None)
    accumulated = jnp.zeros((REQS * T_MAX, D), jnp.float32)
    accumulated, _ = lax.scan(per_expert, accumulated, jnp.arange(EXPERTS, dtype=jnp.int32))
    expert_out = accumulated.reshape(REQS, T_MAX, D).astype(jnp.bfloat16)
    return (final_states, attention_out, expert_out)
```

```python
import functools

import jax
import jax.numpy as jnp
from jax import lax
from jax.experimental import pallas as pl
from jax.experimental.pallas import tpu as pltpu
from jax.sharding import PartitionSpec as P

D = 2304
FF = 512
H = 16
DK = 128
DV = 128
TOP = 8
T_MAX = 16
AXES = ("dev", "side")
HIGHEST = lax.Precision.HIGHEST
VMEM_LIMIT = 48 * 1024 * 1024


def dot_nt(a, b):
    return lax.dot_general(
        a, b, (((1,), (1,)), ((), ())), precision=HIGHEST, preferred_element_type=jnp.float32
    )


def dot_nn(a, b):
    return lax.dot_general(
        a, b, (((1,), (0,)), ((), ())), precision=HIGHEST, preferred_element_type=jnp.float32
    )


def dot_tn(a, b):
    return lax.dot_general(
        a, b, (((0,), (0,)), ((), ())), precision=HIGHEST, preferred_element_type=jnp.float32
    )


def pack_kernel(scalars, states_ref, send_ref, keep_ref):
    for out_ref, base in ((send_ref, 1), (keep_ref, 3)):
        for member in range(2):
            slot = scalars[base + member]
            value = jnp.zeros(states_ref.shape[2:], jnp.float32)
            for r in range(states_ref.shape[0]):
                value = jnp.where(slot == r, states_ref[r, 0], value)
            out_ref[0, member] = value.astype(jnp.bfloat16)


def unit(vectors):
    return vectors * lax.rsqrt(jnp.sum(vectors * vectors, axis=-1, keepdims=True) + 1e-06)


def prep_kernel(counts, q_ref, k_ref, v_ref, decay_ref, rate_ref, z_ref, uo_ref, dg_ref):
    r = pl.program_id(0)
    count = counts[r]
    times = lax.broadcasted_iota(jnp.int32, (T_MAX, 1), 0)
    live = (times < count).astype(jnp.float32)
    rows = lax.broadcasted_iota(jnp.int32, (T_MAX, T_MAX), 0)
    cols = lax.broadcasted_iota(jnp.int32, (T_MAX, T_MAX), 1)
    lower = (cols <= rows).astype(jnp.float32)
    decay = decay_ref[0] * live
    total = dot_nn(lower, decay)
    rates = rate_ref[0] * live
    for h in range(q_ref.shape[2] // DK):
        lanes = slice(h * DK, (h + 1) * DK)
        cum = total[:, lanes]
        grown = jnp.exp(-cum)
        key = unit(k_ref[0, :, lanes].astype(jnp.float32))
        query = unit(q_ref[0, :, lanes].astype(jnp.float32)) * live
        value = v_ref[0, :, lanes].astype(jnp.float32)
        rate = rates[:, h : h + 1]
        key_in = key * grown
        query_in = query * grown
        key_out = key * jnp.exp(cum)
        gram = dot_nt(jnp.concatenate([key_in, query_in], axis=0), key_out)
        mix = jnp.where(cols < rows, gram[:T_MAX], 0.0) * rate
        read = jnp.where(cols <= rows, gram[T_MAX:], 0.0)
        solved = jnp.concatenate([value, key_in], axis=1) * rate
        for s in range(T_MAX - 1):
            solved = solved - mix[:, s : s + 1] * solved[s : s + 1, :]
        seen = dot_nn(read, solved)
        z_ref[0, h, :T_MAX] = solved[:, DV:]
        z_ref[0, h, T_MAX:] = query_in - seen[:, DV:]
        uo_ref[0, h, :T_MAX] = solved[:, :DV]
        uo_ref[0, h, T_MAX:] = seen[:, :DV]
        last = cum[T_MAX - 1 : T_MAX]
        dg_ref[0, h, :T_MAX] = key * jnp.exp(cum - last)
        dg_ref[0, h, T_MAX:] = jnp.broadcast_to(jnp.exp(-last), (8, DK))


def finish_kernel(pieces, heads, scalars, states_ref, *refs):
    mine = refs[:pieces]
    other = refs[pieces : 2 * pieces]
    z_ref, uo_ref, dg_ref, new_ref, out_ref = refs[2 * pieces :]
    r = pl.program_id(0)
    base = 1 + 3 * r
    moved = scalars[base] > 0
    is_other = scalars[base + 1] > 0

    def whole(parts):
        parts = [part[0, 0] for part in parts]
        return parts[0] if pieces == 1 else jnp.concatenate(parts, axis=0)

    arrived = jnp.where(is_other, whole(other).astype(jnp.float32), whole(mine).astype(jnp.float32))
    for h in range(heads):
        state = jnp.where(moved, arrived[h * DK : (h + 1) * DK], states_ref[0, h])
        both = dot_nn(z_ref[0, h], state)
        writes = uo_ref[0, h, :T_MAX] - both[:T_MAX]
        read = uo_ref[0, h, T_MAX:] + both[T_MAX:]
        out_ref[0, :, h * DV : (h + 1) * DV] = read.astype(out_ref.dtype)
        turned = jnp.transpose(dg_ref[0, h, T_MAX:])
        new_ref[0, h] = turned[:, :1] * state + dot_tn(dg_ref[0, h, :T_MAX], writes)


def per_device(
    states,
    swap_pairs,
    token_counts,
    query_vectors,
    key_vectors,
    value_vectors,
    decay_log,
    write_rate,
    hidden_rows,
    expert_ids,
    route_weights,
    gate_up_weight,
    down_weight,
):
    local_reqs = states.shape[0]
    dev_count = lax.axis_size("dev")
    side_count = lax.axis_size("side")
    peer_count = dev_count * side_count
    position = lax.axis_index(AXES)
    side = lax.axis_index("side")
    dev = lax.axis_index("dev")
    inner = 2
    outer = dev_count // inner
    f32, bf16 = jnp.float32, jnp.bfloat16

    def flip(x, dz=0, dy=0, ds=0):
        pairs = []
        for d in range(dev_count):
            for s in range(side_count):
                to = (((d // inner) ^ dz) * inner + ((d % inner) ^ dy)) * side_count + (s ^ ds)
                pairs.append((d * side_count + s, to))
        return lax.ppermute(x, AXES, pairs)

    row_total = local_reqs * T_MAX
    rows_flat = hidden_rows.reshape(row_total, D)
    ids = expert_ids.reshape(row_total, TOP)
    gates = route_weights.reshape(row_total, TOP)
    experts = jnp.arange(peer_count, dtype=jnp.int32)
    table = jnp.sum(jnp.where(ids[:, :, None] == experts, gates[:, :, None], 0.0), axis=1)
    high = lax.reduce_precision(table, 8, 7)
    low = (table - high).astype(bf16)
    pad = -2 * peer_count % 128
    row = jnp.concatenate(
        [rows_flat, high.astype(bf16), low, jnp.zeros((row_total, pad), bf16)], axis=1
    )
    line = [row] + [flip(row, dz=k) for k in range(1, outer)]
    across = [flip(x, dy=1) for x in line]

    first_slot = position * local_reqs
    blocks = inner * outer
    block_rows = H * DK // blocks
    chip = (dev % inner) * outer + dev // inner
    own_pair = lax.dynamic_index_in_dim(swap_pairs, side, 0, keepdims=False)
    other_pair = lax.dynamic_index_in_dim(swap_pairs, 1 - side, 0, keepdims=False)
    pack_scalars = jnp.concatenate(
        [chip[None], other_pair - first_slot, own_pair - first_slot]
    ).astype(jnp.int32)
    packed = jax.ShapeDtypeStruct((blocks, 2, block_rows, DV), bf16)
    out_spec = pl.BlockSpec((1, 2, block_rows, DV), lambda g, s: (g, 0, 0, 0))
    send, keep = pl.pallas_call(
        pack_kernel,
        out_shape=(packed, packed),
        grid_spec=pltpu.PrefetchScalarGridSpec(
            num_scalar_prefetch=1,
            grid=(blocks,),
            in_specs=[
                pl.BlockSpec(
                    (local_reqs, 1, block_rows, DV), lambda g, s: (0, jnp.bitwise_xor(g, s[0]), 0, 0)
                )
            ],
            out_specs=[out_spec, out_spec],
        ),
        name="pack",
    )(pack_scalars, states.reshape(local_reqs, blocks, block_rows, DV))
    chip_part = keep + flip(send, ds=1)
    line_part = chip_part[:outer] + flip(chip_part[outer:], dy=1)
    piece = line_part[0]
    for k in range(1, outer):
        piece = piece + flip(line_part[k], dz=k)
    half = jnp.stack([piece] + [flip(piece, dz=k) for k in range(1, outer)])
    mine = jnp.concatenate([half, flip(half, dy=1)])
    other = flip(mine, ds=1)

    lanes = H * DK
    vec_spec = pl.BlockSpec((1, T_MAX, lanes), lambda r, c: (r, 0, 0))

    def per_head(n):
        return (
            jax.ShapeDtypeStruct((local_reqs, H, n, DK), f32),
            pl.BlockSpec((1, H, n, DK), lambda r, c: (r, 0, 0, 0)),
        )

    shapes, specs = zip(per_head(2 * T_MAX), per_head(2 * T_MAX), per_head(T_MAX + 8))
    z, uo, dg = pl.pallas_call(
        prep_kernel,
        out_shape=shapes,
        grid_spec=pltpu.PrefetchScalarGridSpec(
            num_scalar_prefetch=1,
            grid=(local_reqs,),
            in_specs=[vec_spec] * 4 + [pl.BlockSpec((1, T_MAX, H), lambda r, c: (r, 0, 0))],
            out_specs=list(specs),
        ),
        compiler_params=pltpu.CompilerParams(vmem_limit_bytes=VMEM_LIMIT),
        name="prep",
    )(token_counts, query_vectors, key_vectors, value_vectors, decay_log, write_rate)

    def feed(x):
        gate = x[:, D:].astype(f32)
        picked = (experts == position).astype(f32)
        weight = jnp.sum(
            (gate[:, :peer_count] + gate[:, peer_count : 2 * peer_count]) * picked, axis=1
        )
        gate_up = jnp.dot(x[:, :D], gate_up_weight[0], preferred_element_type=f32)
        activated = (jax.nn.silu(gate_up[:, :FF]) * gate_up[:, FF:]).astype(bf16)
        produced = jnp.dot(activated, down_weight[0], preferred_element_type=f32)
        return (produced * weight[:, None]).astype(bf16)

    def chip_sum(group):
        n = group.shape[0]
        fed = feed(jnp.concatenate([group, flip(group, ds=1)]))
        return fed[:n].astype(f32) + flip(fed[n:], ds=1).astype(f32)

    near = chip_sum(jnp.concatenate(line))
    far = chip_sum(jnp.concatenate(across)).astype(bf16)

    def chunk(x, k):
        return x[k * row_total : (k + 1) * row_total]

    result = None
    for k in range(outer - 1, -1, -1):
        part = chunk(near, k) + flip(chunk(far, k), dy=1).astype(f32)
        if k:
            part = flip(part.astype(bf16), dz=k).astype(f32)
        result = part if result is None else result + part
    expert_out = result.astype(bf16).reshape(local_reqs, T_MAX, D)

    flat_pairs = jnp.concatenate([own_pair, other_pair])
    my_slots = first_slot + jnp.arange(local_reqs, dtype=jnp.int32)
    match = (my_slots[:, None] == flat_pairs[None, :]).astype(jnp.int32)
    moved = jnp.sum(match, axis=1)
    is_other = jnp.sum(match * jnp.array([0, 0, 1, 1], jnp.int32), axis=1)
    member = jnp.sum(match * jnp.array([1, 0, 1, 0], jnp.int32), axis=1)
    scalars = jnp.concatenate(
        [chip[None], jnp.stack([moved, is_other, member], axis=1).reshape(-1)]
    ).astype(jnp.int32)
    heads = max(1, block_rows // DK)
    pieces = max(1, DK // block_rows)

    def piece_spec(which, j):
        def index(r, g, s):
            used = (s[1 + 3 * r] > 0) & (s[2 + 3 * r] == which)
            at = jnp.bitwise_xor(g * pieces + j, s[0])
            return (jnp.where(used, at, 0), jnp.where(used, s[3 + 3 * r], 0), 0, 0)

        return pl.BlockSpec((1, 1, block_rows, DV), index)

    def head_spec(n):
        return pl.BlockSpec((1, heads, n, DK), lambda r, g, s: (r, g, 0, 0))

    new_states, attention_out = pl.pallas_call(
        functools.partial(finish_kernel, pieces, heads),
        out_shape=(
            jax.ShapeDtypeStruct(states.shape, f32),
            jax.ShapeDtypeStruct(query_vectors.shape, bf16),
        ),
        grid_spec=pltpu.PrefetchScalarGridSpec(
            num_scalar_prefetch=1,
            grid=(local_reqs, H // heads),
            in_specs=[head_spec(DK)]
            + [piece_spec(which, j) for which in range(2) for j in range(pieces)]
            + [head_spec(2 * T_MAX), head_spec(2 * T_MAX), head_spec(T_MAX + 8)],
            out_specs=[
                head_spec(DK),
                pl.BlockSpec((1, T_MAX, heads * DV), lambda r, g, s: (r, 0, g)),
            ],
        ),
        name="finish",
    )(scalars, states, *[mine] * pieces, *[other] * pieces, z, uo, dg)
    return (new_states, attention_out, expert_out)


def solution(mesh):
    slots = P(("groups", "dev", "side"))
    experts = P(("dev", "side"))
    in_specs = (slots, P("groups")) + (slots,) * 9 + (experts, experts)
    return jax.shard_map(
        per_device, mesh=mesh, in_specs=in_specs, out_specs=(slots, slots, slots), check_vma=False
    )
```

```python
import functools

import jax
import jax.numpy as jnp
from jax import lax
from jax.experimental import pallas as pl
from jax.experimental.pallas import tpu as pltpu
from jax.sharding import PartitionSpec as P

D = 2304
FF = 512
H = 16
DK = 128
DV = 128
TOP = 8
T_MAX = 16
AXES = ("dev", "side")
HIGHEST = lax.Precision.HIGHEST
VMEM_LIMIT = 48 * 1024 * 1024


def dot_nt(a, b):
    return lax.dot_general(
        a, b, (((1,), (1,)), ((), ())), precision=HIGHEST, preferred_element_type=jnp.float32
    )


def dot_nn(a, b):
    return lax.dot_general(
        a, b, (((1,), (0,)), ((), ())), precision=HIGHEST, preferred_element_type=jnp.float32
    )


def pack_kernel(scalars, send_in, keep_in, send_ref, keep_ref):
    send_ref[...] = send_in[0].astype(jnp.bfloat16)
    keep_ref[...] = keep_in[0].astype(jnp.bfloat16)


def unit(vectors):
    return vectors * lax.rsqrt(jnp.sum(vectors * vectors, axis=-1, keepdims=True) + 1e-06)


def prep_kernel(
    counts, q_ref, k_ref, v_ref, decay_ref, rate_ref, z_ref, uo_ref, key_ref, kept_ref
):
    r = pl.program_id(0)
    count = counts[r]
    times = lax.broadcasted_iota(jnp.int32, (T_MAX, 1), 0)
    live = (times < count).astype(jnp.float32)
    rows = lax.broadcasted_iota(jnp.int32, (T_MAX, T_MAX), 0)
    cols = lax.broadcasted_iota(jnp.int32, (T_MAX, T_MAX), 1)
    lower = (cols <= rows).astype(jnp.float32)
    decay = decay_ref[0] * live
    total = dot_nn(lower, decay)
    rates = rate_ref[0] * live
    for h in range(q_ref.shape[2] // DK):
        lanes = slice(h * DK, (h + 1) * DK)
        cum = total[:, lanes]
        grown = jnp.exp(-cum)
        key = unit(k_ref[0, :, lanes].astype(jnp.float32))
        query = unit(q_ref[0, :, lanes].astype(jnp.float32)) * live
        value = v_ref[0, :, lanes].astype(jnp.float32)
        rate = rates[:, h : h + 1]
        key_in = key * grown
        query_in = query * grown
        key_out = key * jnp.exp(cum)
        gram = dot_nt(jnp.concatenate([key_in, query_in], axis=0), key_out)
        mix = jnp.where(cols < rows, gram[:T_MAX], 0.0) * rate
        read = jnp.where(cols <= rows, gram[T_MAX:], 0.0)
        solved = jnp.concatenate([value, key_in], axis=1) * rate
        for s in range(T_MAX - 1):
            solved = solved - mix[:, s : s + 1] * solved[s : s + 1, :]
        seen = dot_nn(read, solved)
        high, low = split(jnp.concatenate([solved[:, DV:], query_in - seen[:, DV:]], axis=0))
        z_ref[0, h] = jnp.concatenate([high, high, low], axis=1)
        uo_ref[0, h, :T_MAX] = solved[:, :DV]
        uo_ref[0, h, T_MAX:] = seen[:, :DV]
        last = cum[T_MAX - 1 : T_MAX]
        high, low = split(key * jnp.exp(cum - last))
        key_ref[0, h] = jnp.concatenate([high, high, low], axis=0)
        kept_ref[0, h] = jnp.broadcast_to(jnp.exp(-last), (8, DK))


def split(x):
    high = x.astype(jnp.bfloat16)
    return high, (x - high.astype(jnp.float32)).astype(jnp.bfloat16)


def finish_kernel(
    heads,
    block_rows,
    scalars,
    states_ref,
    mine,
    near,
    other,
    z_ref,
    uo_ref,
    key_ref,
    kept_ref,
    new_ref,
    out_ref,
):
    r = pl.program_id(0)
    first = pl.program_id(1) * heads
    source = scalars[1 + r]
    partner = jnp.where(source == 1, 1 - r, r)
    for h in range(heads):
        row = (first + h) * DK
        block = jnp.bitwise_xor(row // block_rows, scalars[0])
        at = pl.ds(pl.multiple_of(row % block_rows, DK), DK)
        arrived = jnp.where(
            source == 2, mine[block, at], jnp.where(source == 3, near[block, at], other[block, at])
        )
        state = jnp.where(source >= 2, arrived.astype(jnp.float32), states_ref[partner, h])
        high, low = split(state)
        both = jnp.dot(
            z_ref[0, h],
            jnp.concatenate([high, low, high], axis=0),
            preferred_element_type=jnp.float32,
        )
        writes = uo_ref[0, h, :T_MAX] - both[:T_MAX]
        read = uo_ref[0, h, T_MAX:] + both[T_MAX:]
        out_ref[0, :, h * DV : (h + 1) * DV] = read.astype(out_ref.dtype)
        high, low = split(writes)
        written = lax.dot_general(
            key_ref[0, h],
            jnp.concatenate([high, low, high], axis=0),
            (((0,), (0,)), ((), ())),
            preferred_element_type=jnp.float32,
        )
        new_ref[0, h] = jnp.transpose(kept_ref[0, h])[:, :1] * state + written


def per_device(
    states,
    swap_pairs,
    token_counts,
    query_vectors,
    key_vectors,
    value_vectors,
    decay_log,
    write_rate,
    hidden_rows,
    expert_ids,
    route_weights,
    gate_up_weight,
    down_weight,
):
    local_reqs = states.shape[0]
    dev_count = lax.axis_size("dev")
    side_count = lax.axis_size("side")
    peer_count = dev_count * side_count
    position = lax.axis_index(AXES)
    side = lax.axis_index("side")
    dev = lax.axis_index("dev")
    inner = 2
    outer = dev_count // inner
    masks = []
    while len(masks) == 0 or masks[-1] + 1 < outer:
        masks.append(2 ** (len(masks) + 1) - 1)
    f32, bf16 = jnp.float32, jnp.bfloat16

    def flip(x, dz=0, dy=0, ds=0):
        pairs = []
        for d in range(dev_count):
            for s in range(side_count):
                to = (((d // inner) ^ dz) * inner + ((d % inner) ^ dy)) * side_count + (s ^ ds)
                pairs.append((d * side_count + s, to))
        return lax.ppermute(x, AXES, pairs)

    def after(x, *earlier):
        return lax.optimization_barrier((x, *earlier))[0]

    row_total = local_reqs * T_MAX
    rows_flat = hidden_rows.reshape(row_total, D)
    ids = expert_ids.reshape(row_total, TOP)
    gates = route_weights.reshape(row_total, TOP)
    experts = jnp.arange(peer_count, dtype=jnp.int32)
    table = jnp.sum(jnp.where(ids[:, :, None] == experts, gates[:, :, None], 0.0), axis=1)
    high = lax.reduce_precision(table, 8, 7)
    low = (table - high).astype(bf16)
    pad = -2 * peer_count % 128
    row = jnp.concatenate(
        [rows_flat, high.astype(bf16), low, jnp.zeros((row_total, pad), bf16)], axis=1
    )
    line = [row]
    across = [flip(row, dy=1)]
    for mask in reversed(masks):
        fresh = [flip(x, dz=mask) for x in line]
        across = across + [flip(x, dy=1) for x in fresh]
        line = line + fresh

    first_slot = position * local_reqs
    blocks = dev_count // 2
    block_rows = H * DK // blocks
    line_at = dev // inner
    gray = line_at ^ (line_at >> 1)
    chip = dev % inner
    for bit in range(len(masks) - 1):
        chip = chip * 2 + (gray >> bit) % 2
    owners = swap_pairs // local_reqs
    slot_in = swap_pairs % local_reqs
    local_pair = owners[:, 0] == owners[:, 1]
    owned = owners == position
    held_slot = jnp.where(owned[:, 0], slot_in[:, 0], slot_in[:, 1])
    pair = side
    pick = jnp.stack([chip, held_slot[1 - pair], held_slot[pair]]).astype(jnp.int32)

    def state_spec(which):
        return pl.BlockSpec(
            (1, 1, block_rows, DV), lambda g, s: (s[which], jnp.bitwise_xor(g, s[0]), 0, 0)
        )

    packed = jax.ShapeDtypeStruct((blocks, block_rows, DV), bf16)
    out_spec = pl.BlockSpec((1, block_rows, DV), lambda g, s: (g, 0, 0))
    state_blocks = states.reshape(local_reqs, blocks, block_rows, DV)
    send, keep = pl.pallas_call(
        pack_kernel,
        out_shape=(packed, packed),
        grid_spec=pltpu.PrefetchScalarGridSpec(
            num_scalar_prefetch=1,
            grid=(blocks,),
            in_specs=[state_spec(1), state_spec(2)],
            out_specs=[out_spec, out_spec],
        ),
        name="pack",
    )(pick, state_blocks, state_blocks)
    homes = lax.dynamic_index_in_dim(owners, pair, 0, keepdims=False)
    one, two = homes[0], homes[1]
    from_core = flip(send, ds=1)
    held = jnp.where((one == position) | (two == position), keep, from_core)
    cube = [(dev, one // side_count, two // side_count, dict(dy=1))]
    for mask in masks:
        me, x, y, _ = cube[-1]
        cube.append((me // 2, x // 2, y // 2, dict(dz=mask)))
    up = []
    for me, x, y, way in cube[:-1]:
        n = held.shape[0] // 2
        came = flip(held[n:], **way)
        apart = (x // 2 == y // 2) & (x // 2 == me // 2) & (x != y)
        up.append((held[:n], came, apart, way))
        held = jnp.where((x == me) | (y == me), held[:n], came)
    needed = flip(held, **cube[-1][3])
    for own_half, came, apart, way in reversed(up):
        back = flip(jnp.where(apart, own_half, needed), **way)
        needed = jnp.concatenate([jnp.where(apart, came, needed), back])
    cores_apart = (one // side_count == dev) & (two // side_count == dev) & (one != two)
    other = flip(jnp.where(cores_apart, keep, needed), ds=1)

    lanes = H * DK
    vec_spec = pl.BlockSpec((1, T_MAX, lanes), lambda r, c: (r, 0, 0))

    per_head = [
        (2 * T_MAX, 3 * DK, bf16),
        (2 * T_MAX, DV, f32),
        (3 * T_MAX, DK, bf16),
        (8, DK, f32),
    ]
    prepared = pl.pallas_call(
        prep_kernel,
        out_shape=[jax.ShapeDtypeStruct((local_reqs, H, n, m), t) for n, m, t in per_head],
        grid_spec=pltpu.PrefetchScalarGridSpec(
            num_scalar_prefetch=1,
            grid=(local_reqs,),
            in_specs=[vec_spec] * 4 + [pl.BlockSpec((1, T_MAX, H), lambda r, c: (r, 0, 0))],
            out_specs=[
                pl.BlockSpec((1, H, n, m), lambda r, c: (r, 0, 0, 0)) for n, m, t in per_head
            ],
        ),
        compiler_params=pltpu.CompilerParams(vmem_limit_bytes=VMEM_LIMIT),
        name="prep",
    )(token_counts, query_vectors, key_vectors, value_vectors, decay_log, write_rate)

    def feed(x):
        gate = x[:, D:].astype(f32)
        picked = (experts == position).astype(f32)
        weight = jnp.sum(
            (gate[:, :peer_count] + gate[:, peer_count : 2 * peer_count]) * picked, axis=1
        )
        gate_up = jnp.dot(x[:, :D], gate_up_weight[0], preferred_element_type=f32)
        activated = (jax.nn.silu(gate_up[:, :FF]) * gate_up[:, FF:]).astype(bf16)
        produced = jnp.dot(activated, down_weight[0], preferred_element_type=f32)
        return (produced * weight[:, None]).astype(bf16)

    def chip_sum(group):
        n = group.shape[0]
        fed = feed(jnp.concatenate([group, flip(group, ds=1)]))
        return fed[:n].astype(f32) + flip(fed[n:], ds=1).astype(f32)

    near = chip_sum(jnp.concatenate(line))
    far = chip_sum(jnp.concatenate(across)).astype(bf16)

    def chunk(x, k):
        return x[k * row_total : (k + 1) * row_total]

    def total_of(k, level):
        if level == 0:
            return chunk(near, k) + flip(chunk(far, k), dy=1).astype(f32)
        n = outer >> level
        mask = masks[level - 1]
        return total_of(k, level - 1) + flip(
            total_of(k + n, level - 1).astype(bf16), dz=mask
        ).astype(f32)

    expert_out = total_of(0, len(masks)).astype(bf16).reshape(local_reqs, T_MAX, D)

    my_slots = first_slot + jnp.arange(local_reqs, dtype=jnp.int32)
    match = my_slots[:, None, None] == swap_pairs[None]
    mine_pair = jnp.arange(side_count, dtype=jnp.int32) == pair
    kind = jnp.where(local_pair, 1, jnp.where(mine_pair, jnp.where(cores_apart, 3, 2), 4))
    source = jnp.sum(jnp.where(match, kind[None, :, None], 0), axis=(1, 2))
    scalars = jnp.concatenate([chip[None], source]).astype(jnp.int32)
    heads = H // 2

    def head_spec(n, m):
        return pl.BlockSpec((1, heads, n, m), lambda r, g, s: (r, g, 0, 0))

    piece_spec = pl.BlockSpec((blocks, block_rows, DV), lambda r, g, s: (0, 0, 0))
    new_states, attention_out = pl.pallas_call(
        functools.partial(finish_kernel, heads, block_rows),
        out_shape=(
            jax.ShapeDtypeStruct(states.shape, f32),
            jax.ShapeDtypeStruct(query_vectors.shape, bf16),
        ),
        grid_spec=pltpu.PrefetchScalarGridSpec(
            num_scalar_prefetch=1,
            grid=(local_reqs, H // heads),
            in_specs=[pl.BlockSpec((local_reqs, heads, DK, DV), lambda r, g, s: (0, g, 0, 0))]
            + [piece_spec] * 3
            + [head_spec(n, m) for n, m, _ in per_head],
            out_specs=[
                head_spec(DK, DV),
                pl.BlockSpec((1, T_MAX, heads * DV), lambda r, g, s: (r, 0, g)),
            ],
        ),
        compiler_params=pltpu.CompilerParams(vmem_limit_bytes=VMEM_LIMIT),
        name="finish",
    )(scalars, states, needed, from_core, other, *prepared)
    return (new_states, attention_out, expert_out)


def solution(mesh):
    slots = P(("groups", "dev", "side"))
    experts = P(("dev", "side"))
    in_specs = (slots, P("groups")) + (slots,) * 9 + (experts, experts)
    return jax.shard_map(
        per_device, mesh=mesh, in_specs=in_specs, out_specs=(slots, slots, slots), check_vma=False
    )
```

```python
import functools

import jax
import jax.numpy as jnp
from jax import lax
from jax.experimental import pallas as pl
from jax.experimental.pallas import tpu as pltpu
from jax.sharding import PartitionSpec as P

D = 2304
FF = 512
H = 16
DK = 128
DV = 128
TOP = 8
T_MAX = 16
AXES = ("dev", "side")
HIGHEST = lax.Precision.HIGHEST
VMEM_LIMIT = 48 * 1024 * 1024


def dot_nt(a, b):
    return lax.dot_general(
        a, b, (((1,), (1,)), ((), ())), precision=HIGHEST, preferred_element_type=jnp.float32
    )


def dot_nn(a, b):
    return lax.dot_general(
        a, b, (((1,), (0,)), ((), ())), precision=HIGHEST, preferred_element_type=jnp.float32
    )


def rows_kernel(experts, hidden_ref, ids_ref, gates_ref, out_ref):
    width = out_ref.shape[1] - D
    for r in range(hidden_ref.shape[0]):
        here = slice(r * T_MAX, (r + 1) * T_MAX)
        out_ref[here, :D] = hidden_ref[r]
        number = lax.broadcasted_iota(jnp.int32, (experts, T_MAX), 0)
        table = jnp.zeros((experts, T_MAX), jnp.float32)
        for k in range(TOP):
            table = jnp.where(ids_ref[r, k : k + 1] == number, gates_ref[r, k : k + 1], table)
        high = table.astype(jnp.bfloat16).astype(jnp.float32)
        parts = [high, table - high]
        if width > 2 * experts:
            parts.append(jnp.zeros((width - 2 * experts, T_MAX), jnp.float32))
        out_ref[here, D:] = jnp.transpose(jnp.concatenate(parts, axis=0)).astype(jnp.bfloat16)


def chip_of(position, sides, bits):
    dev = lax.div(position, sides)
    line_at = lax.shift_right_logical(dev, 1)
    gray = jnp.bitwise_xor(line_at, lax.shift_right_logical(line_at, 1))
    chip = jnp.bitwise_and(dev, 1)
    for bit in range(bits):
        chip = chip * 2 + jnp.bitwise_and(lax.shift_right_logical(gray, bit), 1)
    return chip


def pack_kernel(sides, slots, levels, swaps, where_at, send_in, keep_in, send_ref, keep_ref, plan):
    send_ref[...] = send_in[0].astype(jnp.bfloat16)
    keep_ref[...] = keep_in[0].astype(jnp.bfloat16)

    @pl.when(pl.program_id(0) == 0)
    def _():
        position = where_at[0]
        pair = lax.rem(position, sides)
        one = lax.div(swaps[pair, 0], slots)
        two = lax.div(swaps[pair, 1], slots)
        me = lax.div(position, sides)
        x = lax.div(one, sides)
        y = lax.div(two, sides)
        flags = [(one == position) | (two == position), (x == me) & (y == me) & (one != two)]
        for level in range(levels):
            near = (x == me) | (y == me)
            differ = x != y
            x, y, me = x >> 1, y >> 1, me >> 1
            flags.extend([differ & (x == me) & (y == me), near])
        row = lax.broadcasted_iota(jnp.int32, plan.shape, 0)
        value = jnp.zeros(plan.shape, jnp.int32)
        for i, flag in enumerate(flags):
            value = jnp.where(row == i, flag.astype(jnp.int32), value)
        plan[...] = value.astype(jnp.float32).astype(plan.dtype)


def unit(vectors):
    return vectors * lax.rsqrt(jnp.sum(vectors * vectors, axis=-1, keepdims=True) + 1e-06)


def prep_kernel(
    counts, q_ref, k_ref, v_ref, decay_ref, rate_ref, z_ref, uo_ref, key_ref, kept_ref
):
    r = pl.program_id(0)
    count = counts[r]
    times = lax.broadcasted_iota(jnp.int32, (T_MAX, 1), 0)
    live = (times < count).astype(jnp.float32)
    rows = lax.broadcasted_iota(jnp.int32, (T_MAX, T_MAX), 0)
    cols = lax.broadcasted_iota(jnp.int32, (T_MAX, T_MAX), 1)
    lower = (cols <= rows).astype(jnp.float32)
    decay = decay_ref[0] * live
    total = dot_nn(lower, decay)
    rates = rate_ref[0] * live
    for h in range(q_ref.shape[2] // DK):
        lanes = slice(h * DK, (h + 1) * DK)
        cum = total[:, lanes]
        grown = jnp.exp(-cum)
        key = unit(k_ref[0, :, lanes].astype(jnp.float32))
        query = unit(q_ref[0, :, lanes].astype(jnp.float32)) * live
        value = v_ref[0, :, lanes].astype(jnp.float32)
        rate = rates[:, h : h + 1]
        key_in = key * grown
        query_in = query * grown
        key_out = key * jnp.exp(cum)
        gram = dot_nt(jnp.concatenate([key_in, query_in], axis=0), key_out)
        mix = jnp.where(cols < rows, gram[:T_MAX], 0.0) * rate
        read = jnp.where(cols <= rows, gram[T_MAX:], 0.0)
        solved = jnp.concatenate([value, key_in], axis=1) * rate
        for s in range(T_MAX - 1):
            solved = solved - mix[:, s : s + 1] * solved[s : s + 1, :]
        seen = dot_nn(read, solved)
        high, low = split(jnp.concatenate([solved[:, DV:], query_in - seen[:, DV:]], axis=0))
        z_ref[0, h] = jnp.concatenate([high, high, low], axis=1)
        uo_ref[0, h, :T_MAX] = solved[:, :DV]
        uo_ref[0, h, T_MAX:] = seen[:, :DV]
        last = cum[T_MAX - 1 : T_MAX]
        high, low = split(key * jnp.exp(cum - last))
        key_ref[0, h] = jnp.concatenate([high, high, low], axis=0)
        kept_ref[0, h] = jnp.broadcast_to(jnp.exp(-last), (8, DK))


def split(x):
    high = x.astype(jnp.bfloat16)
    return high, (x - high.astype(jnp.float32)).astype(jnp.bfloat16)


def finish_kernel(
    heads,
    block_rows,
    sides,
    bits,
    swaps,
    where_at,
    states_ref,
    mine,
    near,
    other,
    z_ref,
    uo_ref,
    key_ref,
    kept_ref,
    new_ref,
    out_ref,
):
    r = pl.program_id(0)
    first = pl.program_id(1) * heads
    position = where_at[0]
    slots = states_ref.shape[0]
    chip = chip_of(position, sides, bits)
    source = jnp.int32(0)
    for p in range(swaps.shape[0]):
        one = lax.div(swaps[p, 0], slots)
        two = lax.div(swaps[p, 1], slots)
        apart = lax.div(one, sides) == lax.div(two, sides)
        kind = jnp.where(lax.rem(position, sides) == p, jnp.where(apart, 3, 2), 4)
        kind = jnp.where(one == two, 1, kind)
        slot = position * slots + r
        source = jnp.where((swaps[p, 0] == slot) | (swaps[p, 1] == slot), kind, source)
    partner = jnp.where(source == 1, 1 - r, r)
    for h in range(heads):
        row = (first + h) * DK
        block = jnp.bitwise_xor(lax.div(row, block_rows), chip)
        at = pl.ds(pl.multiple_of(lax.rem(row, block_rows), DK), DK)
        arrived = jnp.where(
            source == 2, mine[block, at], jnp.where(source == 3, near[block, at], other[block, at])
        )
        state = jnp.where(source >= 2, arrived.astype(jnp.float32), states_ref[partner, h])
        high, low = split(state)
        both = jnp.dot(
            z_ref[0, h],
            jnp.concatenate([high, low, high], axis=0),
            preferred_element_type=jnp.float32,
        )
        writes = uo_ref[0, h, :T_MAX] - both[:T_MAX]
        read = uo_ref[0, h, T_MAX:] + both[T_MAX:]
        out_ref[0, :, h * DV : (h + 1) * DV] = read.astype(out_ref.dtype)
        high, low = split(writes)
        written = lax.dot_general(
            key_ref[0, h],
            jnp.concatenate([high, low, high], axis=0),
            (((0,), (0,)), ((), ())),
            preferred_element_type=jnp.float32,
        )
        new_ref[0, h] = jnp.transpose(kept_ref[0, h])[:, :1] * state + written


def per_device(
    states,
    swap_pairs,
    token_counts,
    query_vectors,
    key_vectors,
    value_vectors,
    decay_log,
    write_rate,
    hidden_rows,
    expert_ids,
    route_weights,
    gate_up_weight,
    down_weight,
):
    local_reqs = states.shape[0]
    dev_count = lax.axis_size("dev")
    side_count = lax.axis_size("side")
    peer_count = dev_count * side_count
    position = lax.axis_index(AXES)
    inner = 2
    outer = dev_count // inner
    masks = []
    while len(masks) == 0 or masks[-1] + 1 < outer:
        masks.append(2 ** (len(masks) + 1) - 1)
    f32, bf16 = jnp.float32, jnp.bfloat16

    def flip(x, dz=0, dy=0, ds=0):
        pairs = []
        for d in range(dev_count):
            for s in range(side_count):
                to = (((d // inner) ^ dz) * inner + ((d % inner) ^ dy)) * side_count + (s ^ ds)
                pairs.append((d * side_count + s, to))
        return lax.ppermute(x, AXES, pairs)

    row_total = local_reqs * T_MAX
    experts = jnp.arange(peer_count, dtype=jnp.int32)
    width = D + -(-2 * peer_count // 128) * 128
    row = pl.pallas_call(
        functools.partial(rows_kernel, peer_count),
        out_shape=jax.ShapeDtypeStruct((row_total, width), bf16),
        name="rows",
    )(hidden_rows, jnp.swapaxes(expert_ids, 1, 2), jnp.swapaxes(route_weights, 1, 2))
    def together(*values):
        return lax.optimization_barrier(values)

    line = [row]
    across = [flip(row, dy=1)]
    direct = [flip(row, dz=mask) for mask in reversed(masks)]

    blocks = dev_count // 2
    block_rows = H * DK // blocks
    levels = len(masks)
    here = position.astype(jnp.int32).reshape(1)

    def state_spec(own):
        def index(g, swaps, at):
            pair = lax.rem(at[0], side_count)
            pair = pair if own else 1 - pair
            one, two = swaps[pair, 0], swaps[pair, 1]
            held = jnp.where(lax.div(one, local_reqs) == at[0], one, two)
            chip = chip_of(at[0], side_count, levels - 1)
            return (lax.rem(held, local_reqs), jnp.bitwise_xor(g, chip), 0, 0)

        return pl.BlockSpec((1, 1, block_rows, DV), index)

    packed = jax.ShapeDtypeStruct((blocks, block_rows, DV), bf16)
    out_spec = pl.BlockSpec((1, block_rows, DV), lambda g, swaps, at: (g, 0, 0))
    state_blocks = states.reshape(local_reqs, blocks, block_rows, DV)
    send, keep, plan = pl.pallas_call(
        functools.partial(pack_kernel, side_count, local_reqs, levels),
        out_shape=(packed, packed, jax.ShapeDtypeStruct((16, DV), bf16)),
        grid_spec=pltpu.PrefetchScalarGridSpec(
            num_scalar_prefetch=2,
            grid=(blocks,),
            in_specs=[state_spec(False), state_spec(True)],
            out_specs=[out_spec, out_spec, pl.BlockSpec((16, DV), lambda g, swaps, at: (0, 0))],
        ),
        name="pack",
    )(swap_pairs, here, state_blocks, state_blocks)
    from_core = flip(send, ds=1)

    def choose(flag, yes, no):
        return jnp.where(plan[flag] > 0, yes, no)

    held = choose(0, keep, from_core)
    direct[0], held = together(direct[0], held)
    for i, mask in enumerate(reversed(masks)):
        fresh = direct[i : i + 1] + [flip(x, dz=mask) for x in line[1:]]
        across = across + [flip(x, dy=1) for x in fresh]
        line = line + fresh

    lanes = H * DK
    vec_spec = pl.BlockSpec((1, T_MAX, lanes), lambda r, c: (r, 0, 0))

    per_head = [
        (2 * T_MAX, 3 * DK, bf16),
        (2 * T_MAX, DV, f32),
        (3 * T_MAX, DK, bf16),
        (8, DK, f32),
    ]
    counts, line[-1] = together(token_counts, line[-1])
    prepared = pl.pallas_call(
        prep_kernel,
        out_shape=[jax.ShapeDtypeStruct((local_reqs, H, n, m), t) for n, m, t in per_head],
        grid_spec=pltpu.PrefetchScalarGridSpec(
            num_scalar_prefetch=1,
            grid=(local_reqs,),
            in_specs=[vec_spec] * 4 + [pl.BlockSpec((1, T_MAX, H), lambda r, c: (r, 0, 0))],
            out_specs=[
                pl.BlockSpec((1, H, n, m), lambda r, c: (r, 0, 0, 0)) for n, m, t in per_head
            ],
        ),
        compiler_params=pltpu.CompilerParams(vmem_limit_bytes=VMEM_LIMIT),
        name="prep",
    )(counts, query_vectors, key_vectors, value_vectors, decay_log, write_rate)

    ways = [dict(dy=1)] + [dict(dz=mask) for mask in masks]
    up = []
    for level in range(levels):
        n = held.shape[0] // 2
        came = flip(held[n:], **ways[level])
        if level == 0:
            came, *prepared = lax.optimization_barrier((came, *prepared))
        up.append((held[:n], came))
        held = choose(3 + 2 * level, held[:n], came)
    needed = flip(held, **ways[levels])
    def feed(x):
        gate = x[:, D:].astype(f32)
        picked = (experts == position).astype(f32)
        weight = jnp.sum(
            (gate[:, :peer_count] + gate[:, peer_count : 2 * peer_count]) * picked, axis=1
        )
        gate_up = jnp.dot(x[:, :D], gate_up_weight[0], preferred_element_type=f32)
        activated = (jax.nn.silu(gate_up[:, :FF]) * gate_up[:, FF:]).astype(bf16)
        produced = jnp.dot(activated, down_weight[0], preferred_element_type=f32)
        return (produced * weight[:, None]).astype(bf16)

    def chip_sum(group):
        n = group.shape[0]
        fed = feed(jnp.concatenate([group, flip(group, ds=1)]))
        return fed[:n].astype(f32) + flip(fed[n:], ds=1).astype(f32)

    near = chip_sum(jnp.concatenate(line))
    far = chip_sum(jnp.concatenate(across)).astype(bf16)
    needed, far = together(needed, far)

    for level in range(levels - 1, -1, -1):
        own_half, came = up[level]
        back = flip(choose(2 + 2 * level, own_half, needed), **ways[level])
        needed = jnp.concatenate([choose(2 + 2 * level, came, needed), back])
    other = flip(choose(1, keep, needed), ds=1)

    def chunk(x, k):
        return x[k * row_total : (k + 1) * row_total]

    def total_of(k, level):
        if level == 0:
            return chunk(near, k) + flip(chunk(far, k), dy=1).astype(f32)
        n = outer >> level
        mask = masks[level - 1]
        return total_of(k, level - 1) + flip(
            total_of(k + n, level - 1).astype(bf16), dz=mask
        ).astype(f32)

    expert_out = total_of(0, len(masks)).astype(bf16).reshape(local_reqs, T_MAX, D)

    heads = H // 2

    def head_spec(n, m):
        return pl.BlockSpec((1, heads, n, m), lambda r, g, swaps, at: (r, g, 0, 0))

    piece_spec = pl.BlockSpec((blocks, block_rows, DV), lambda r, g, swaps, at: (0, 0, 0))
    new_states, attention_out = pl.pallas_call(
        functools.partial(finish_kernel, heads, block_rows, side_count, levels - 1),
        out_shape=(
            jax.ShapeDtypeStruct(states.shape, f32),
            jax.ShapeDtypeStruct(query_vectors.shape, bf16),
        ),
        grid_spec=pltpu.PrefetchScalarGridSpec(
            num_scalar_prefetch=2,
            grid=(local_reqs, H // heads),
            in_specs=[pl.BlockSpec((local_reqs, heads, DK, DV), lambda r, g, swaps, at: (0, g, 0, 0))]
            + [piece_spec] * 3
            + [head_spec(n, m) for n, m, _ in per_head],
            out_specs=[
                head_spec(DK, DV),
                pl.BlockSpec((1, T_MAX, heads * DV), lambda r, g, swaps, at: (r, 0, g)),
            ],
        ),
        compiler_params=pltpu.CompilerParams(vmem_limit_bytes=VMEM_LIMIT),
        name="finish",
    )(swap_pairs, here, states, needed, from_core, other, *prepared)
    return (new_states, attention_out, expert_out)


def solution(mesh):
    slots = P(("groups", "dev", "side"))
    experts = P(("dev", "side"))
    in_specs = (slots, P("groups")) + (slots,) * 9 + (experts, experts)
    return jax.shard_map(
        per_device, mesh=mesh, in_specs=in_specs, out_specs=(slots, slots, slots), check_vma=False
    )
```

```python
import functools

import jax
import jax.numpy as jnp
from jax import lax
from jax.experimental import pallas as pl
from jax.experimental.pallas import tpu as pltpu
from jax.sharding import PartitionSpec as P

D = 2304
FF = 512
H = 16
DK = 128
DV = 128
TOP = 8
T_MAX = 16
AXES = ("dev", "side")
HIGHEST = lax.Precision.HIGHEST
VMEM_LIMIT = 16 * 1024 * 1024


def dot_nt(a, b):
    return lax.dot_general(
        a, b, (((1,), (1,)), ((), ())), precision=HIGHEST, preferred_element_type=jnp.float32
    )


def dot_nn(a, b):
    return lax.dot_general(
        a, b, (((1,), (0,)), ((), ())), precision=HIGHEST, preferred_element_type=jnp.float32
    )


def rows_kernel(experts, hidden_ref, ids_ref, gates_ref, out_ref):
    width = out_ref.shape[1] - D
    for r in range(hidden_ref.shape[0]):
        here = slice(r * T_MAX, (r + 1) * T_MAX)
        out_ref[here, :D] = hidden_ref[r]
        number = lax.broadcasted_iota(jnp.int32, (experts, T_MAX), 0)
        table = jnp.zeros((experts, T_MAX), jnp.float32)
        for k in range(TOP):
            table = jnp.where(ids_ref[r, k : k + 1] == number, gates_ref[r, k : k + 1], table)
        high = table.astype(jnp.bfloat16).astype(jnp.float32)
        parts = [high, table - high]
        if width > 2 * experts:
            parts.append(jnp.zeros((width - 2 * experts, T_MAX), jnp.float32))
        out_ref[here, D:] = jnp.transpose(jnp.concatenate(parts, axis=0)).astype(jnp.bfloat16)


def chip_of(position, sides, bits):
    dev = lax.div(position, sides)
    line_at = lax.shift_right_logical(dev, 1)
    gray = jnp.bitwise_xor(line_at, lax.shift_right_logical(line_at, 1))
    chip = jnp.bitwise_and(dev, 1)
    for bit in range(bits):
        chip = chip * 2 + jnp.bitwise_and(lax.shift_right_logical(gray, bit), 1)
    return chip


def pack_kernel(sides, slots, levels, swaps, where_at, send_in, keep_in, send_ref, keep_ref, plan):
    count = send_ref.shape[0]
    swapped = lax.rem(chip_of(where_at[0], sides, levels - 1), count)
    for k in range(count):
        send_ref[k] = send_in[0, jnp.bitwise_xor(swapped, k)].astype(jnp.bfloat16)
        keep_ref[k] = keep_in[0, jnp.bitwise_xor(swapped, k)].astype(jnp.bfloat16)

    @pl.when(pl.program_id(0) == 0)
    def _():
        position = where_at[0]
        pair = lax.rem(position, sides)
        one = lax.div(swaps[pair, 0], slots)
        two = lax.div(swaps[pair, 1], slots)
        me = lax.div(position, sides)
        x = lax.div(one, sides)
        y = lax.div(two, sides)
        flags = [(one == position) | (two == position), (x == me) & (y == me) & (one != two)]
        for level in range(levels):
            near = (x == me) | (y == me)
            differ = x != y
            x, y, me = x >> 1, y >> 1, me >> 1
            flags.extend([differ & (x == me) & (y == me), near])
        row = lax.broadcasted_iota(jnp.int32, plan.shape, 0)
        value = jnp.zeros(plan.shape, jnp.int32)
        for i, flag in enumerate(flags):
            value = jnp.where(row == i, flag.astype(jnp.int32), value)
        plan[...] = value.astype(jnp.float32).astype(plan.dtype)


def unit(vectors):
    return vectors * lax.rsqrt(jnp.sum(vectors * vectors, axis=-1, keepdims=True) + 1e-06)


def prep_kernel(
    counts, q_ref, k_ref, v_ref, decay_ref, rate_ref, z_ref, uo_ref, key_ref, kept_ref
):
    r = pl.program_id(0)
    count = counts[r]
    times = lax.broadcasted_iota(jnp.int32, (T_MAX, 1), 0)
    live = (times < count).astype(jnp.float32)
    rows = lax.broadcasted_iota(jnp.int32, (T_MAX, T_MAX), 0)
    cols = lax.broadcasted_iota(jnp.int32, (T_MAX, T_MAX), 1)
    lower = (cols <= rows).astype(jnp.float32)
    decay = decay_ref[0] * live
    total = dot_nn(lower, decay)
    rates = rate_ref[0] * live
    for h in range(q_ref.shape[2] // DK):
        lanes = slice(h * DK, (h + 1) * DK)
        cum = total[:, lanes]
        grown = jnp.exp(-cum)
        key = unit(k_ref[0, :, lanes].astype(jnp.float32))
        query = unit(q_ref[0, :, lanes].astype(jnp.float32)) * live
        value = v_ref[0, :, lanes].astype(jnp.float32)
        rate = rates[:, h : h + 1]
        key_in = key * grown
        query_in = query * grown
        key_out = key * jnp.exp(cum)
        gram = dot_nt(jnp.concatenate([key_in, query_in], axis=0), key_out)
        mix = jnp.where(cols < rows, gram[:T_MAX], 0.0) * rate
        read = jnp.where(cols <= rows, gram[T_MAX:], 0.0)
        solved = jnp.concatenate([value, key_in], axis=1) * rate
        for s in range(T_MAX - 1):
            solved = solved - mix[:, s : s + 1] * solved[s : s + 1, :]
        seen = dot_nn(read, solved)
        high, low = split(jnp.concatenate([solved[:, DV:], query_in - seen[:, DV:]], axis=0))
        z_ref[0, h] = jnp.concatenate([high, low], axis=0)
        uo_ref[0, h, :T_MAX] = solved[:, :DV]
        uo_ref[0, h, T_MAX:] = seen[:, :DV]
        last = cum[T_MAX - 1 : T_MAX]
        high, low = split(key * jnp.exp(cum - last))
        key_ref[0, h] = jnp.concatenate([high, high, low], axis=0)
        kept_ref[0, h] = jnp.broadcast_to(jnp.exp(-last), (8, DK))


def split(x):
    high = x.astype(jnp.bfloat16)
    return high, (x - high.astype(jnp.float32)).astype(jnp.bfloat16)


def finish_kernel(
    heads,
    block_rows,
    sides,
    bits,
    swaps,
    where_at,
    states_ref,
    mine,
    near,
    other,
    z_ref,
    uo_ref,
    key_ref,
    kept_ref,
    new_ref,
    out_ref,
):
    r = pl.program_id(0)
    first = pl.program_id(1) * heads
    position = where_at[0]
    slots = states_ref.shape[0]
    chip = chip_of(position, sides, bits)
    source = jnp.int32(0)
    for p in range(swaps.shape[0]):
        one = lax.div(swaps[p, 0], slots)
        two = lax.div(swaps[p, 1], slots)
        apart = lax.div(one, sides) == lax.div(two, sides)
        kind = jnp.where(lax.rem(position, sides) == p, jnp.where(apart, 3, 2), 4)
        kind = jnp.where(one == two, 1, kind)
        slot = position * slots + r
        source = jnp.where((swaps[p, 0] == slot) | (swaps[p, 1] == slot), kind, source)
    partner = jnp.where(source == 1, 1 - r, r)
    for h in range(heads):
        row = (first + h) * DK
        block = jnp.bitwise_xor(lax.div(row, block_rows), chip)
        at = pl.ds(pl.multiple_of(lax.rem(row, block_rows), DK), DK)
        arrived = jnp.where(
            source == 2, mine[block, at], jnp.where(source == 3, near[block, at], other[block, at])
        )
        state = jnp.where(source >= 2, arrived.astype(jnp.float32), states_ref[partner, h])
        both = jnp.dot(z_ref[0, h], state.astype(jnp.bfloat16), preferred_element_type=jnp.float32)
        both = both[: 2 * T_MAX] + both[2 * T_MAX :]
        writes = uo_ref[0, h, :T_MAX] - both[:T_MAX]
        read = uo_ref[0, h, T_MAX:] + both[T_MAX:]
        out_ref[0, :, h * DV : (h + 1) * DV] = read.astype(out_ref.dtype)
        high, low = split(writes)
        written = lax.dot_general(
            key_ref[0, h],
            jnp.concatenate([high, low, high], axis=0),
            (((0,), (0,)), ((), ())),
            preferred_element_type=jnp.float32,
        )
        new_ref[0, h] = jnp.transpose(kept_ref[0, h])[:, :1] * state + written


def per_device(
    states,
    swap_pairs,
    token_counts,
    query_vectors,
    key_vectors,
    value_vectors,
    decay_log,
    write_rate,
    hidden_rows,
    expert_ids,
    route_weights,
    gate_up_weight,
    down_weight,
):
    local_reqs = states.shape[0]
    dev_count = lax.axis_size("dev")
    side_count = lax.axis_size("side")
    peer_count = dev_count * side_count
    position = lax.axis_index(AXES)
    inner = 2
    outer = dev_count // inner
    masks = []
    while len(masks) == 0 or masks[-1] + 1 < outer:
        masks.append(2 ** (len(masks) + 1) - 1)
    f32, bf16 = jnp.float32, jnp.bfloat16

    def flip(x, dz=0, dy=0, ds=0):
        pairs = []
        for d in range(dev_count):
            for s in range(side_count):
                to = (((d // inner) ^ dz) * inner + ((d % inner) ^ dy)) * side_count + (s ^ ds)
                pairs.append((d * side_count + s, to))
        return lax.ppermute(x, AXES, pairs)

    row_total = local_reqs * T_MAX
    experts = jnp.arange(peer_count, dtype=jnp.int32)
    width = D + -(-2 * peer_count // 128) * 128
    row = pl.pallas_call(
        functools.partial(rows_kernel, peer_count),
        out_shape=jax.ShapeDtypeStruct((row_total, width), bf16),
        name="rows",
    )(hidden_rows, jnp.swapaxes(expert_ids, 1, 2), jnp.swapaxes(route_weights, 1, 2))
    def together(*values):
        return lax.optimization_barrier(values)

    line = [row]
    across = [flip(row, dy=1)]
    direct = [flip(row, dz=mask) for mask in reversed(masks)]

    blocks = dev_count // 2
    block_rows = H * DK // blocks
    levels = len(masks)
    here = position.astype(jnp.int32).reshape(1)

    def state_spec(own):
        def index(g, swaps, at):
            pair = lax.rem(at[0], side_count)
            pair = pair if own else 1 - pair
            one, two = swaps[pair, 0], swaps[pair, 1]
            held = jnp.where(lax.div(one, local_reqs) == at[0], one, two)
            across_at = jnp.bitwise_and(lax.div(at[0], side_count), 1)
            return (lax.rem(held, local_reqs), jnp.bitwise_xor(g, across_at), 0, 0)

        return pl.BlockSpec((1, blocks // 2, block_rows, DV), index)

    packed = jax.ShapeDtypeStruct((blocks, block_rows, DV), bf16)
    out_spec = pl.BlockSpec((blocks // 2, block_rows, DV), lambda g, swaps, at: (g, 0, 0))
    state_blocks = states.reshape(local_reqs, blocks, block_rows, DV)
    send, keep, plan = pl.pallas_call(
        functools.partial(pack_kernel, side_count, local_reqs, levels),
        out_shape=(packed, packed, jax.ShapeDtypeStruct((16, DV), bf16)),
        grid_spec=pltpu.PrefetchScalarGridSpec(
            num_scalar_prefetch=2,
            grid=(2,),
            in_specs=[state_spec(False), state_spec(True)],
            out_specs=[out_spec, out_spec, pl.BlockSpec((16, DV), lambda g, swaps, at: (0, 0))],
        ),
        name="pack",
    )(swap_pairs, here, state_blocks, state_blocks)
    from_core = flip(send, ds=1)

    def choose(flag, yes, no):
        return jnp.where(plan[flag] > 0, yes, no)

    held = choose(0, keep, from_core)
    direct[0], held = together(direct[0], held)
    for i, mask in enumerate(reversed(masks)):
        fresh = direct[i : i + 1] + [flip(x, dz=mask) for x in line[1:]]
        if i == 0:
            across = across + [flip(x, dy=1) for x in fresh]
        else:
            across = across + [
                flip(across[k], dz=mask) if k % 2 == 0 else flip(fresh[k], dy=1)
                for k in range(len(fresh))
            ]
        line = line + fresh

    lanes = H * DK
    vec_spec = pl.BlockSpec((1, T_MAX, lanes), lambda r, c: (r, 0, 0))

    per_head = [
        (4 * T_MAX, DK, bf16),
        (2 * T_MAX, DV, f32),
        (3 * T_MAX, DK, bf16),
        (8, DK, f32),
    ]
    counts = together(token_counts, across[1])[0]
    prepared = pl.pallas_call(
        prep_kernel,
        out_shape=[jax.ShapeDtypeStruct((local_reqs, H, n, m), t) for n, m, t in per_head],
        grid_spec=pltpu.PrefetchScalarGridSpec(
            num_scalar_prefetch=1,
            grid=(local_reqs,),
            in_specs=[vec_spec] * 4 + [pl.BlockSpec((1, T_MAX, H), lambda r, c: (r, 0, 0))],
            out_specs=[
                pl.BlockSpec((1, H, n, m), lambda r, c: (r, 0, 0, 0)) for n, m, t in per_head
            ],
        ),
        compiler_params=pltpu.CompilerParams(vmem_limit_bytes=VMEM_LIMIT),
        name="prep",
    )(counts, query_vectors, key_vectors, value_vectors, decay_log, write_rate)

    ways = [dict(dy=1)] + [dict(dz=mask) for mask in masks]
    up = []
    for level in range(levels):
        n = held.shape[0] // 2
        came = flip(held[n:], **ways[level])
        if level == 0:
            came, *prepared = together(came, *prepared)
        up.append((held[:n], came))
        held = choose(3 + 2 * level, held[:n], came)
    needed = flip(held, **ways[levels])
    def feed(x):
        gate = x[:, D:].astype(f32)
        picked = (experts == position).astype(f32)
        weight = jnp.sum(
            (gate[:, :peer_count] + gate[:, peer_count : 2 * peer_count]) * picked, axis=1
        )
        gate_up = jnp.dot(x[:, :D], gate_up_weight[0], preferred_element_type=f32)
        activated = (jax.nn.silu(gate_up[:, :FF]) * gate_up[:, FF:]).astype(bf16)
        produced = jnp.dot(activated, down_weight[0], preferred_element_type=f32)
        return (produced * weight[:, None]).astype(bf16)

    def chip_feed(group):
        return feed(jnp.concatenate([group, flip(group, ds=1)]))

    def chip_sum(fed):
        n = fed.shape[0] // 2
        return fed[:n].astype(f32) + flip(fed[n:], ds=1).astype(f32)

    near = chip_feed(jnp.concatenate(line))
    across[-1], near = together(across[-1], near)
    far = chip_sum(chip_feed(jnp.concatenate(across))).astype(bf16)
    near = chip_sum(near)
    needed = together(needed, far)[0]

    for level in range(levels - 1, -1, -1):
        own_half, came = up[level]
        back = flip(choose(2 + 2 * level, own_half, needed), **ways[level])
        needed = jnp.concatenate([choose(2 + 2 * level, came, needed), back])
    other = flip(choose(1, keep, needed), ds=1)

    def chunk(x, k):
        return x[k * row_total : (k + 1) * row_total]

    def along(parts):
        for mask in masks[:-1]:
            n = len(parts) // 2
            parts = [
                parts[k].astype(f32) + flip(parts[k + n].astype(bf16), dz=mask).astype(f32)
                for k in range(n)
            ]
        return parts[0].astype(f32)

    crossed = [
        chunk(near, k) + flip(chunk(far, k), dy=1).astype(f32) for k in range(1, outer, 2)
    ]
    near_sum = along([chunk(near, k) for k in range(0, outer, 2)])
    far_sum = along([chunk(far, k) for k in range(0, outer, 2)])
    own_sum = near_sum + flip(far_sum.astype(bf16), dy=1).astype(f32)
    mirrored = flip(along(crossed).astype(bf16), dz=masks[-1])

    heads = H // 2

    def head_spec(n, m):
        return pl.BlockSpec((1, heads, n, m), lambda r, g, swaps, at: (r, g, 0, 0))

    piece_spec = pl.BlockSpec((blocks, block_rows, DV), lambda r, g, swaps, at: (0, 0, 0))
    new_states, attention_out = pl.pallas_call(
        functools.partial(finish_kernel, heads, block_rows, side_count, levels - 1),
        out_shape=(
            jax.ShapeDtypeStruct(states.shape, f32),
            jax.ShapeDtypeStruct(query_vectors.shape, bf16),
        ),
        grid_spec=pltpu.PrefetchScalarGridSpec(
            num_scalar_prefetch=2,
            grid=(local_reqs, H // heads),
            in_specs=[pl.BlockSpec((local_reqs, heads, DK, DV), lambda r, g, swaps, at: (0, g, 0, 0))]
            + [piece_spec] * 3
            + [head_spec(n, m) for n, m, _ in per_head],
            out_specs=[
                head_spec(DK, DV),
                pl.BlockSpec((1, T_MAX, heads * DV), lambda r, g, swaps, at: (r, 0, g)),
            ],
        ),
        compiler_params=pltpu.CompilerParams(vmem_limit_bytes=VMEM_LIMIT),
        name="finish",
    )(swap_pairs, here, states, needed, from_core, other, *prepared)
    mirrored = together(mirrored, attention_out)[0]
    expert_out = (own_sum + mirrored.astype(f32)).astype(bf16).reshape(local_reqs, T_MAX, D)
    return (new_states, attention_out, expert_out)


def solution(mesh):
    slots = P(("groups", "dev", "side"))
    experts = P(("dev", "side"))
    in_specs = (slots, P("groups")) + (slots,) * 9 + (experts, experts)
    return jax.shard_map(
        per_device, mesh=mesh, in_specs=in_specs, out_specs=(slots, slots, slots), check_vma=False
    )
```

```python
import functools

import jax
import jax.numpy as jnp
from jax import lax
from jax.experimental import pallas as pl
from jax.experimental.pallas import tpu as pltpu
from jax.sharding import PartitionSpec as P

D = 2304
FF = 512
H = 16
DK = 128
DV = 128
TOP = 8
T_MAX = 16
AXES = ("dev", "side")
HIGHEST = lax.Precision.HIGHEST
VMEM_LIMIT = 16 * 1024 * 1024


def dot_nt(a, b):
    return lax.dot_general(
        a, b, (((1,), (1,)), ((), ())), precision=HIGHEST, preferred_element_type=jnp.float32
    )


def dot_nn(a, b):
    return lax.dot_general(
        a, b, (((1,), (0,)), ((), ())), precision=HIGHEST, preferred_element_type=jnp.float32
    )


def rows_kernel(experts, hidden_ref, ids_ref, gates_ref, out_ref):
    width = out_ref.shape[1] - D
    for r in range(hidden_ref.shape[0]):
        here = slice(r * T_MAX, (r + 1) * T_MAX)
        out_ref[here, :D] = hidden_ref[r]
        number = lax.broadcasted_iota(jnp.int32, (experts, T_MAX), 0)
        table = jnp.zeros((experts, T_MAX), jnp.float32)
        for k in range(TOP):
            table = jnp.where(ids_ref[r, k : k + 1] == number, gates_ref[r, k : k + 1], table)
        high = table.astype(jnp.bfloat16).astype(jnp.float32)
        parts = [high, table - high]
        if width > 2 * experts:
            parts.append(jnp.zeros((width - 2 * experts, T_MAX), jnp.float32))
        out_ref[here, D:] = jnp.transpose(jnp.concatenate(parts, axis=0)).astype(jnp.bfloat16)


def chip_of(position, sides, bits):
    dev = lax.div(position, sides)
    line_at = lax.shift_right_logical(dev, 1)
    gray = jnp.bitwise_xor(line_at, lax.shift_right_logical(line_at, 1))
    chip = jnp.bitwise_and(dev, 1)
    for bit in range(bits):
        chip = chip * 2 + jnp.bitwise_and(lax.shift_right_logical(gray, bit), 1)
    return chip


def pack_kernel(sides, slots, levels, swaps, where_at, send_in, keep_in, send_ref, keep_ref, plan):
    count = send_ref.shape[0]
    swapped = lax.rem(chip_of(where_at[0], sides, levels - 1), count)
    for k in range(count):
        send_ref[k] = send_in[0, jnp.bitwise_xor(swapped, k)].astype(jnp.bfloat16)
        keep_ref[k] = keep_in[0, jnp.bitwise_xor(swapped, k)].astype(jnp.bfloat16)

    @pl.when(pl.program_id(0) == 0)
    def _():
        position = where_at[0]
        pair = lax.rem(position, sides)
        one = lax.div(swaps[pair, 0], slots)
        two = lax.div(swaps[pair, 1], slots)
        me = lax.div(position, sides)
        x = lax.div(one, sides)
        y = lax.div(two, sides)
        flags = [(one == position) | (two == position), (x == me) & (y == me) & (one != two)]
        for level in range(levels):
            near = (x == me) | (y == me)
            differ = x != y
            x, y, me = x >> 1, y >> 1, me >> 1
            flags.extend([differ & (x == me) & (y == me), near])
        row = lax.broadcasted_iota(jnp.int32, plan.shape, 0)
        value = jnp.zeros(plan.shape, jnp.int32)
        for i, flag in enumerate(flags):
            value = jnp.where(row == i, flag.astype(jnp.int32), value)
        plan[...] = value.astype(jnp.float32).astype(plan.dtype)


def unit(vectors):
    return vectors * lax.rsqrt(jnp.sum(vectors * vectors, axis=-1, keepdims=True) + 1e-06)


def fetch_and_prep_kernel(r, counts, weight_ref, *refs):
    fetch = pltpu.make_async_copy(weight_ref, refs[-2], refs[-1])
    fetch.start()
    prep_kernel(r, counts, *refs[:-2])
    fetch.wait()


def prep_kernel(r, counts, q_ref, k_ref, v_ref, decay_ref, rate_ref, *refs):
    z_ref, uo_ref, key_ref, kept_ref = refs[-4:]
    count = counts[r]
    times = lax.broadcasted_iota(jnp.int32, (T_MAX, 1), 0)
    live = (times < count).astype(jnp.float32)
    rows = lax.broadcasted_iota(jnp.int32, (T_MAX, T_MAX), 0)
    cols = lax.broadcasted_iota(jnp.int32, (T_MAX, T_MAX), 1)
    lower = (cols <= rows).astype(jnp.float32)
    decay = decay_ref[0] * live
    total = dot_nn(lower, decay)
    rates = rate_ref[0] * live
    for h in range(q_ref.shape[2] // DK):
        lanes = slice(h * DK, (h + 1) * DK)
        cum = total[:, lanes]
        grown = jnp.exp(-cum)
        key = unit(k_ref[0, :, lanes].astype(jnp.float32))
        query = unit(q_ref[0, :, lanes].astype(jnp.float32)) * live
        value = v_ref[0, :, lanes].astype(jnp.float32)
        rate = rates[:, h : h + 1]
        key_in = key * grown
        query_in = query * grown
        key_out = key * jnp.exp(cum)
        gram = dot_nt(jnp.concatenate([key_in, query_in], axis=0), key_out)
        mix = jnp.where(cols < rows, gram[:T_MAX], 0.0) * rate
        read = jnp.where(cols <= rows, gram[T_MAX:], 0.0)
        solved = jnp.concatenate([value, key_in], axis=1) * rate
        for s in range(T_MAX - 1):
            solved = solved - mix[:, s : s + 1] * solved[s : s + 1, :]
        seen = dot_nn(read, solved)
        high, low = split(jnp.concatenate([solved[:, DV:], query_in - seen[:, DV:]], axis=0))
        z_ref[0, h] = jnp.concatenate([high, low], axis=0)
        uo_ref[0, h, :T_MAX] = solved[:, :DV]
        uo_ref[0, h, T_MAX:] = seen[:, :DV]
        last = cum[T_MAX - 1 : T_MAX]
        high, low = split(key * jnp.exp(cum - last))
        key_ref[0, h] = jnp.concatenate([high, high, low], axis=0)
        kept_ref[0, h] = jnp.broadcast_to(jnp.exp(-last), (8, DK))


def split(x):
    high = x.astype(jnp.bfloat16)
    return high, (x - high.astype(jnp.float32)).astype(jnp.bfloat16)


def finish_kernel(
    heads,
    block_rows,
    sides,
    bits,
    swaps,
    where_at,
    states_ref,
    mine,
    near,
    other,
    z_ref,
    uo_ref,
    key_ref,
    kept_ref,
    new_ref,
    out_ref,
):
    r = pl.program_id(0)
    first = pl.program_id(1) * heads
    position = where_at[0]
    slots = z_ref.shape[0]
    chip = chip_of(position, sides, bits)
    source = jnp.int32(0)
    for p in range(swaps.shape[0]):
        one = lax.div(swaps[p, 0], slots)
        two = lax.div(swaps[p, 1], slots)
        apart = lax.div(one, sides) == lax.div(two, sides)
        kind = jnp.where(lax.rem(position, sides) == p, jnp.where(apart, 3, 2), 4)
        kind = jnp.where(one == two, 1, kind)
        slot = position * slots + r
        source = jnp.where((swaps[p, 0] == slot) | (swaps[p, 1] == slot), kind, source)
    for h in range(heads):
        row = (first + h) * DK
        block = jnp.bitwise_xor(lax.div(row, block_rows), chip)
        at = pl.ds(pl.multiple_of(lax.rem(row, block_rows), DK), DK)
        arrived = jnp.where(
            source == 2, mine[block, at], jnp.where(source == 3, near[block, at], other[block, at])
        )
        state = jnp.where(source >= 2, arrived.astype(jnp.float32), states_ref[0, h])
        both = jnp.dot(z_ref[r, first + h], state.astype(jnp.bfloat16), preferred_element_type=jnp.float32)
        both = both[: 2 * T_MAX] + both[2 * T_MAX :]
        writes = uo_ref[r, first + h, :T_MAX] - both[:T_MAX]
        read = uo_ref[r, first + h, T_MAX:] + both[T_MAX:]
        out_ref[0, :, h * DV : (h + 1) * DV] = read.astype(out_ref.dtype)
        high, low = split(writes)
        written = lax.dot_general(
            key_ref[r, first + h],
            jnp.concatenate([high, low, high], axis=0),
            (((0,), (0,)), ((), ())),
            preferred_element_type=jnp.float32,
        )
        new_ref[0, h] = jnp.transpose(kept_ref[r, first + h])[:, :1] * state + written


def per_device(
    states,
    swap_pairs,
    token_counts,
    query_vectors,
    key_vectors,
    value_vectors,
    decay_log,
    write_rate,
    hidden_rows,
    expert_ids,
    route_weights,
    gate_up_weight,
    down_weight,
):
    local_reqs = states.shape[0]
    dev_count = lax.axis_size("dev")
    side_count = lax.axis_size("side")
    peer_count = dev_count * side_count
    position = lax.axis_index(AXES)
    inner = 2
    outer = dev_count // inner
    masks = []
    while len(masks) == 0 or masks[-1] + 1 < outer:
        masks.append(2 ** (len(masks) + 1) - 1)
    f32, bf16 = jnp.float32, jnp.bfloat16

    def flip(x, dz=0, dy=0, ds=0):
        pairs = []
        for d in range(dev_count):
            for s in range(side_count):
                to = (((d // inner) ^ dz) * inner + ((d % inner) ^ dy)) * side_count + (s ^ ds)
                pairs.append((d * side_count + s, to))
        return lax.ppermute(x, AXES, pairs)

    row_total = local_reqs * T_MAX
    experts = jnp.arange(peer_count, dtype=jnp.int32)
    width = D + -(-2 * peer_count // 128) * 128
    row = pl.pallas_call(
        functools.partial(rows_kernel, peer_count),
        out_shape=jax.ShapeDtypeStruct((row_total, width), bf16),
        name="rows",
    )(hidden_rows, jnp.swapaxes(expert_ids, 1, 2), jnp.swapaxes(route_weights, 1, 2))
    def together(*values):
        return lax.optimization_barrier(values)

    line = [row]
    across = [flip(row, dy=1)]
    direct = [flip(row, dz=mask) for mask in reversed(masks)]

    blocks = dev_count // 2
    block_rows = H * DK // blocks
    levels = len(masks)
    here = position.astype(jnp.int32).reshape(1)

    def state_spec(own):
        def index(g, swaps, at):
            pair = lax.rem(at[0], side_count)
            pair = pair if own else 1 - pair
            one, two = swaps[pair, 0], swaps[pair, 1]
            held = jnp.where(lax.div(one, local_reqs) == at[0], one, two)
            across_at = jnp.bitwise_and(lax.div(at[0], side_count), 1)
            return (lax.rem(held, local_reqs), jnp.bitwise_xor(g, across_at), 0, 0)

        return pl.BlockSpec((1, blocks // 2, block_rows, DV), index)

    packed = jax.ShapeDtypeStruct((blocks, block_rows, DV), bf16)
    out_spec = pl.BlockSpec((blocks // 2, block_rows, DV), lambda g, swaps, at: (g, 0, 0))
    state_blocks = states.reshape(local_reqs, blocks, block_rows, DV)
    send, keep, plan = pl.pallas_call(
        functools.partial(pack_kernel, side_count, local_reqs, levels),
        out_shape=(packed, packed, jax.ShapeDtypeStruct((16, DV), bf16)),
        grid_spec=pltpu.PrefetchScalarGridSpec(
            num_scalar_prefetch=2,
            grid=(2,),
            in_specs=[state_spec(False), state_spec(True)],
            out_specs=[out_spec, out_spec, pl.BlockSpec((16, DV), lambda g, swaps, at: (0, 0))],
        ),
        compiler_params=pltpu.CompilerParams(vmem_limit_bytes=VMEM_LIMIT),
        name="pack",
    )(swap_pairs, here, state_blocks, state_blocks)
    from_core = flip(send, ds=1)

    lanes = H * DK
    per_head = [
        (4 * T_MAX, DK, bf16),
        (2 * T_MAX, DV, f32),
        (3 * T_MAX, DK, bf16),
        (8, DK, f32),
    ]

    def prepare(r, counts, weight=None, earlier=()):
        anywhere = [pl.BlockSpec(memory_space=pl.ANY)]
        fetched = [] if weight is None else [weight]
        return pl.pallas_call(
            functools.partial(fetch_and_prep_kernel if fetched else prep_kernel, r),
            out_shape=[jax.ShapeDtypeStruct((local_reqs, H, n, m), t) for n, m, t in per_head]
            + fetched,
            grid_spec=pltpu.PrefetchScalarGridSpec(
                num_scalar_prefetch=1,
                grid=(1,),
                in_specs=anywhere * len(fetched)
                + [pl.BlockSpec((1, T_MAX, lanes), lambda g, c: (r, 0, 0))] * 4
                + [pl.BlockSpec((1, T_MAX, H), lambda g, c: (r, 0, 0))]
                + anywhere * len(earlier),
                out_specs=[
                    pl.BlockSpec((1, H, n, m), lambda g, c: (r, 0, 0, 0)) for n, m, t in per_head
                ]
                + anywhere * len(fetched),
                scratch_shapes=[pltpu.SemaphoreType.DMA] * len(fetched),
            ),
            input_output_aliases={6 + len(fetched) + i: i for i in range(len(earlier))},
            compiler_params=pltpu.CompilerParams(vmem_limit_bytes=VMEM_LIMIT),
            name=f"prep{r}",
        )(
            counts,
            *fetched,
            query_vectors,
            key_vectors,
            value_vectors,
            decay_log,
            write_rate,
            *earlier,
        )

    def choose(flag, yes, no):
        return jnp.where(plan[flag] > 0, yes, no)

    held = choose(0, keep, from_core)
    direct[0], held = together(direct[0], held)
    counts, = together(token_counts, held)[:1]
    prepared = prepare(0, counts)
    for i, mask in enumerate(reversed(masks)):
        fresh = direct[i : i + 1] + [flip(x, dz=mask) for x in line[1:]]
        if i == levels - 1:
            fresh[-1], *prepared = together(fresh[-1], *prepared)
        if i == 0:
            across = across + [flip(x, dy=1) for x in fresh]
        else:
            across = across + [
                flip(across[k], dz=mask) if k % 2 == 0 else flip(fresh[k], dy=1)
                for k in range(len(fresh))
            ]
        line = line + fresh

    counts = together(token_counts, across[1])[0]
    *prepared, first_weight = prepare(1, counts, gate_up_weight[0], prepared)
    ways = [dict(dy=1)] + [dict(dz=mask) for mask in masks]
    up = []
    for level in range(levels):
        n = held.shape[0] // 2
        came = flip(held[n:], **ways[level])
        if level == 0:
            came, *prepared = together(came, *prepared)
        up.append((held[:n], came))
        held = choose(3 + 2 * level, held[:n], came)
    needed = flip(held, **ways[levels])
    def feed(x):
        gate = x[:, D:].astype(f32)
        picked = (experts == position).astype(f32)
        weight = jnp.sum(
            (gate[:, :peer_count] + gate[:, peer_count : 2 * peer_count]) * picked, axis=1
        )
        gate_up = jnp.dot(x[:, :D], first_weight, preferred_element_type=f32)
        activated = (jax.nn.silu(gate_up[:, :FF]) * gate_up[:, FF:]).astype(bf16)
        produced = jnp.dot(activated, down_weight[0], preferred_element_type=f32)
        return (produced * weight[:, None]).astype(bf16)

    def chip_feed(group):
        return feed(jnp.concatenate([group, flip(group, ds=1)]))

    def chip_sum(fed):
        n = fed.shape[0] // 2
        return fed[:n].astype(f32) + flip(fed[n:], ds=1).astype(f32)

    near = chip_feed(jnp.concatenate(line))
    across[-1], near = together(across[-1], near)
    far = chip_sum(chip_feed(jnp.concatenate(across))).astype(bf16)
    near = chip_sum(near)
    needed = together(needed, far)[0]

    for level in range(levels - 1, -1, -1):
        own_half, came = up[level]
        back = flip(choose(2 + 2 * level, own_half, needed), **ways[level])
        needed = jnp.concatenate([choose(2 + 2 * level, came, needed), back])
    other = flip(choose(1, keep, needed), ds=1)

    def chunk(x, k):
        return x[k * row_total : (k + 1) * row_total]

    def along(parts):
        for mask in masks[:-1]:
            n = len(parts) // 2
            parts = [
                parts[k].astype(f32) + flip(parts[k + n].astype(bf16), dz=mask).astype(f32)
                for k in range(n)
            ]
        return parts[0].astype(f32)

    arrived = [flip(chunk(far, k), dy=1) for k in range(1, outer, 2)]
    crossed = [chunk(near, k) + arrived[k // 2].astype(f32) for k in range(1, outer, 2)]
    near_sum = along([chunk(near, k) for k in range(0, outer, 2)])
    far_later = together(far, arrived[-1])[0]
    far_sum = along([chunk(far_later, k) for k in range(0, outer, 2)])
    own_sum = near_sum + flip(far_sum.astype(bf16), dy=1).astype(f32)
    mirrored = flip(along(crossed).astype(bf16), dz=masks[-1])

    heads = H // 2

    def head_spec(n, m):
        return pl.BlockSpec((1, heads, n, m), lambda r, g, swaps, at: (r, g, 0, 0))

    resident = pl.BlockSpec(memory_space=pltpu.VMEM)

    def state_index(r, g, swaps, at):
        inside = jnp.bool_(False)
        for p in range(side_count):
            one, two = lax.div(swaps[p, 0], local_reqs), lax.div(swaps[p, 1], local_reqs)
            inside = inside | ((one == at[0]) & (two == at[0]))
        return (jnp.where(inside, local_reqs - 1 - r, r), g, 0, 0)

    new_states, attention_out = pl.pallas_call(
        functools.partial(finish_kernel, heads, block_rows, side_count, levels - 1),
        out_shape=(
            jax.ShapeDtypeStruct(states.shape, f32),
            jax.ShapeDtypeStruct(query_vectors.shape, bf16),
        ),
        grid_spec=pltpu.PrefetchScalarGridSpec(
            num_scalar_prefetch=2,
            grid=(local_reqs, H // heads),
            in_specs=[pl.BlockSpec((1, heads, DK, DV), state_index)] + [resident] * 7,
            out_specs=[
                head_spec(DK, DV),
                pl.BlockSpec((1, T_MAX, heads * DV), lambda r, g, swaps, at: (r, 0, g)),
            ],
        ),
        compiler_params=pltpu.CompilerParams(vmem_limit_bytes=VMEM_LIMIT),
        name="finish",
    )(swap_pairs, here, states, needed, from_core, other, *prepared)
    mirrored = together(mirrored, attention_out)[0]
    expert_out = (own_sum + mirrored.astype(f32)).astype(bf16).reshape(local_reqs, T_MAX, D)
    return (new_states, attention_out, expert_out)


def solution(mesh):
    slots = P(("groups", "dev", "side"))
    experts = P(("dev", "side"))
    in_specs = (slots, P("groups")) + (slots,) * 9 + (experts, experts)
    return jax.shard_map(
        per_device, mesh=mesh, in_specs=in_specs, out_specs=(slots, slots, slots), check_vma=False
    )
```

```python
import functools

import jax
import jax.numpy as jnp
from jax import lax
from jax.experimental import pallas as pl
from jax.experimental.pallas import tpu as pltpu
from jax.sharding import PartitionSpec as P

D = 2304
FF = 512
H = 16
DK = 128
DV = 128
TOP = 8
T_MAX = 16
AXES = ("dev", "side")
HIGHEST = lax.Precision.HIGHEST
VMEM_LIMIT = 16 * 1024 * 1024


def dot_nt(a, b):
    return lax.dot_general(
        a, b, (((1,), (1,)), ((), ())), precision=HIGHEST, preferred_element_type=jnp.float32
    )


def dot_nn(a, b):
    return lax.dot_general(
        a, b, (((1,), (0,)), ((), ())), precision=HIGHEST, preferred_element_type=jnp.float32
    )


def rows_kernel(experts, hidden_ref, ids_ref, gates_ref, out_ref):
    width = out_ref.shape[1] - D
    for r in range(hidden_ref.shape[0]):
        here = slice(r * T_MAX, (r + 1) * T_MAX)
        out_ref[here, :D] = hidden_ref[r]
        number = lax.broadcasted_iota(jnp.int32, (experts, T_MAX), 0)
        table = jnp.zeros((experts, T_MAX), jnp.float32)
        for k in range(TOP):
            table = jnp.where(ids_ref[r, k : k + 1] == number, gates_ref[r, k : k + 1], table)
        high = table.astype(jnp.bfloat16).astype(jnp.float32)
        parts = [high, table - high]
        if width > 2 * experts:
            parts.append(jnp.zeros((width - 2 * experts, T_MAX), jnp.float32))
        out_ref[here, D:] = jnp.transpose(jnp.concatenate(parts, axis=0)).astype(jnp.bfloat16)


def chip_of(position, sides, bits):
    dev = lax.div(position, sides)
    line_at = lax.shift_right_logical(dev, 1)
    gray = jnp.bitwise_xor(line_at, lax.shift_right_logical(line_at, 1))
    chip = jnp.bitwise_and(dev, 1)
    for bit in range(bits):
        chip = chip * 2 + jnp.bitwise_and(lax.shift_right_logical(gray, bit), 1)
    return chip


def pack_kernel(sides, slots, levels, swaps, where_at, send_in, keep_in, send_ref, keep_ref, plan):
    count = send_ref.shape[0]
    swapped = lax.rem(chip_of(where_at[0], sides, levels - 1), count)
    for k in range(count):
        send_ref[k] = send_in[0, jnp.bitwise_xor(swapped, k)].astype(jnp.bfloat16)
        keep_ref[k] = keep_in[0, jnp.bitwise_xor(swapped, k)].astype(jnp.bfloat16)

    @pl.when(pl.program_id(0) == 0)
    def _():
        position = where_at[0]
        pair = lax.rem(position, sides)
        one = lax.div(swaps[pair, 0], slots)
        two = lax.div(swaps[pair, 1], slots)
        me = lax.div(position, sides)
        x = lax.div(one, sides)
        y = lax.div(two, sides)
        flags = [(one == position) | (two == position), (x == me) & (y == me) & (one != two)]
        for level in range(levels):
            near = (x == me) | (y == me)
            differ = x != y
            x, y, me = x >> 1, y >> 1, me >> 1
            flags.extend([differ & (x == me) & (y == me), near])
        row = lax.broadcasted_iota(jnp.int32, plan.shape, 0)
        value = jnp.zeros(plan.shape, jnp.int32)
        for i, flag in enumerate(flags):
            value = jnp.where(row == i, flag.astype(jnp.int32), value)
        plan[...] = value.astype(jnp.float32).astype(plan.dtype)


def unit(vectors):
    return vectors * lax.rsqrt(jnp.sum(vectors * vectors, axis=-1, keepdims=True) + 1e-06)


def fetch_and_prep_kernel(r, counts, weight_ref, *refs):
    fetch = pltpu.make_async_copy(weight_ref, refs[-2], refs[-1])
    fetch.start()
    prep_kernel(r, counts, *refs[:-2])
    fetch.wait()


def prep_kernel(r, counts, q_ref, k_ref, v_ref, decay_ref, rate_ref, *refs):
    z_ref, uo_ref, key_ref, kept_ref = refs[-4:]
    count = counts[r]
    times = lax.broadcasted_iota(jnp.int32, (T_MAX, 1), 0)
    live = (times < count).astype(jnp.float32)
    rows = lax.broadcasted_iota(jnp.int32, (T_MAX, T_MAX), 0)
    cols = lax.broadcasted_iota(jnp.int32, (T_MAX, T_MAX), 1)
    lower = (cols <= rows).astype(jnp.float32)
    decay = decay_ref[0] * live
    total = dot_nn(lower, decay)
    rates = rate_ref[0] * live
    for h in range(q_ref.shape[2] // DK):
        lanes = slice(h * DK, (h + 1) * DK)
        cum = total[:, lanes]
        grown = jnp.exp(-cum)
        key = unit(k_ref[0, :, lanes].astype(jnp.float32))
        query = unit(q_ref[0, :, lanes].astype(jnp.float32)) * live
        value = v_ref[0, :, lanes].astype(jnp.float32)
        rate = rates[:, h : h + 1]
        key_in = key * grown
        query_in = query * grown
        key_out = key * jnp.exp(cum)
        gram = dot_nt(jnp.concatenate([key_in, query_in], axis=0), key_out)
        mix = jnp.where(cols < rows, gram[:T_MAX], 0.0) * rate
        read = jnp.where(cols <= rows, gram[T_MAX:], 0.0)
        solved = jnp.concatenate([value, key_in], axis=1) * rate
        for s in range(T_MAX - 1):
            solved = solved - mix[:, s : s + 1] * solved[s : s + 1, :]
        seen = dot_nn(read, solved)
        high, low = split(jnp.concatenate([solved[:, DV:], query_in - seen[:, DV:]], axis=0))
        z_ref[0, h] = jnp.concatenate([high, low], axis=0)
        uo_ref[0, h, :T_MAX] = solved[:, :DV]
        uo_ref[0, h, T_MAX:] = seen[:, :DV]
        last = cum[T_MAX - 1 : T_MAX]
        high, low = split(key * jnp.exp(cum - last))
        key_ref[0, h] = jnp.concatenate([high, high, low], axis=0)
        kept_ref[0, h] = jnp.broadcast_to(jnp.exp(-last), (8, DK))


def split(x):
    high = x.astype(jnp.bfloat16)
    return high, (x - high.astype(jnp.float32)).astype(jnp.bfloat16)


def finish_kernel(
    heads,
    block_rows,
    sides,
    bits,
    swaps,
    where_at,
    states_ref,
    mine,
    near,
    other,
    z_ref,
    uo_ref,
    key_ref,
    kept_ref,
    new_ref,
    out_ref,
):
    r = pl.program_id(0)
    first = pl.program_id(1) * heads
    position = where_at[0]
    slots = z_ref.shape[0]
    chip = chip_of(position, sides, bits)
    source = jnp.int32(0)
    for p in range(swaps.shape[0]):
        one = lax.div(swaps[p, 0], slots)
        two = lax.div(swaps[p, 1], slots)
        apart = lax.div(one, sides) == lax.div(two, sides)
        kind = jnp.where(lax.rem(position, sides) == p, jnp.where(apart, 3, 2), 4)
        kind = jnp.where(one == two, 1, kind)
        slot = position * slots + r
        source = jnp.where((swaps[p, 0] == slot) | (swaps[p, 1] == slot), kind, source)
    def steps(gathered):
        for h in range(heads):
            row = (first + h) * DK
            block = jnp.bitwise_xor(lax.div(row, block_rows), chip)
            at = pl.ds(pl.multiple_of(lax.rem(row, block_rows), DK), DK)
            state = states_ref[0, h] if gathered is None else gathered[block, at].astype(jnp.float32)
            both = jnp.dot(z_ref[r, first + h], state.astype(jnp.bfloat16), preferred_element_type=jnp.float32)
            both = both[: 2 * T_MAX] + both[2 * T_MAX :]
            writes = uo_ref[r, first + h, :T_MAX] - both[:T_MAX]
            read = uo_ref[r, first + h, T_MAX:] + both[T_MAX:]
            out_ref[0, :, h * DV : (h + 1) * DV] = read.astype(out_ref.dtype)
            high, low = split(writes)
            written = lax.dot_general(
                key_ref[r, first + h],
                jnp.concatenate([high, low, high], axis=0),
                (((0,), (0,)), ((), ())),
                preferred_element_type=jnp.float32,
            )
            new_ref[0, h] = jnp.transpose(kept_ref[r, first + h])[:, :1] * state + written

    for kind, gathered in ((2, mine), (3, near), (4, other)):
        pl.when(source == kind)(functools.partial(steps, gathered))
    pl.when(source < 2)(functools.partial(steps, None))


def per_device(
    states,
    swap_pairs,
    token_counts,
    query_vectors,
    key_vectors,
    value_vectors,
    decay_log,
    write_rate,
    hidden_rows,
    expert_ids,
    route_weights,
    gate_up_weight,
    down_weight,
):
    local_reqs = states.shape[0]
    dev_count = lax.axis_size("dev")
    side_count = lax.axis_size("side")
    peer_count = dev_count * side_count
    position = lax.axis_index(AXES)
    inner = 2
    outer = dev_count // inner
    masks = []
    while len(masks) == 0 or masks[-1] + 1 < outer:
        masks.append(2 ** (len(masks) + 1) - 1)
    f32, bf16 = jnp.float32, jnp.bfloat16

    def flip(x, dz=0, dy=0, ds=0):
        pairs = []
        for d in range(dev_count):
            for s in range(side_count):
                to = (((d // inner) ^ dz) * inner + ((d % inner) ^ dy)) * side_count + (s ^ ds)
                pairs.append((d * side_count + s, to))
        return lax.ppermute(x, AXES, pairs)

    row_total = local_reqs * T_MAX
    experts = jnp.arange(peer_count, dtype=jnp.int32)
    width = D + -(-2 * peer_count // 128) * 128
    row = pl.pallas_call(
        functools.partial(rows_kernel, peer_count),
        out_shape=jax.ShapeDtypeStruct((row_total, width), bf16),
        name="rows",
    )(hidden_rows, jnp.swapaxes(expert_ids, 1, 2), jnp.swapaxes(route_weights, 1, 2))
    def together(*values):
        return lax.optimization_barrier(values)

    line = [row]
    across = [flip(row, dy=1)]
    direct = [flip(row, dz=mask) for mask in reversed(masks)]

    blocks = dev_count // 2
    block_rows = H * DK // blocks
    levels = len(masks)
    here = position.astype(jnp.int32).reshape(1)

    def state_spec(own):
        def index(g, swaps, at):
            pair = lax.rem(at[0], side_count)
            pair = pair if own else 1 - pair
            one, two = swaps[pair, 0], swaps[pair, 1]
            held = jnp.where(lax.div(one, local_reqs) == at[0], one, two)
            across_at = jnp.bitwise_and(lax.div(at[0], side_count), 1)
            return (lax.rem(held, local_reqs), jnp.bitwise_xor(g, across_at), 0, 0)

        return pl.BlockSpec((1, blocks // 2, block_rows, DV), index)

    packed = jax.ShapeDtypeStruct((blocks, block_rows, DV), bf16)
    out_spec = pl.BlockSpec((blocks // 2, block_rows, DV), lambda g, swaps, at: (g, 0, 0))
    state_blocks = states.reshape(local_reqs, blocks, block_rows, DV)
    send, keep, plan = pl.pallas_call(
        functools.partial(pack_kernel, side_count, local_reqs, levels),
        out_shape=(packed, packed, jax.ShapeDtypeStruct((16, DV), bf16)),
        grid_spec=pltpu.PrefetchScalarGridSpec(
            num_scalar_prefetch=2,
            grid=(2,),
            in_specs=[state_spec(False), state_spec(True)],
            out_specs=[out_spec, out_spec, pl.BlockSpec((16, DV), lambda g, swaps, at: (0, 0))],
        ),
        compiler_params=pltpu.CompilerParams(vmem_limit_bytes=VMEM_LIMIT),
        name="pack",
    )(swap_pairs, here, state_blocks, state_blocks)
    from_core = flip(send, ds=1)

    lanes = H * DK
    per_head = [
        (4 * T_MAX, DK, bf16),
        (2 * T_MAX, DV, f32),
        (3 * T_MAX, DK, bf16),
        (8, DK, f32),
    ]

    def prepare(r, counts, weight=None, earlier=()):
        anywhere = [pl.BlockSpec(memory_space=pl.ANY)]
        fetched = [] if weight is None else [weight]
        return pl.pallas_call(
            functools.partial(fetch_and_prep_kernel if fetched else prep_kernel, r),
            out_shape=[jax.ShapeDtypeStruct((local_reqs, H, n, m), t) for n, m, t in per_head]
            + fetched,
            grid_spec=pltpu.PrefetchScalarGridSpec(
                num_scalar_prefetch=1,
                grid=(1,),
                in_specs=anywhere * len(fetched)
                + [pl.BlockSpec((1, T_MAX, lanes), lambda g, c: (r, 0, 0))] * 4
                + [pl.BlockSpec((1, T_MAX, H), lambda g, c: (r, 0, 0))]
                + anywhere * len(earlier),
                out_specs=[
                    pl.BlockSpec((1, H, n, m), lambda g, c: (r, 0, 0, 0)) for n, m, t in per_head
                ]
                + anywhere * len(fetched),
                scratch_shapes=[pltpu.SemaphoreType.DMA] * len(fetched),
            ),
            input_output_aliases={6 + len(fetched) + i: i for i in range(len(earlier))},
            compiler_params=pltpu.CompilerParams(vmem_limit_bytes=VMEM_LIMIT),
            name=f"prep{r}",
        )(
            counts,
            *fetched,
            query_vectors,
            key_vectors,
            value_vectors,
            decay_log,
            write_rate,
            *earlier,
        )

    def choose(flag, yes, no):
        return jnp.where(plan[flag] > 0, yes, no)

    held = choose(0, keep, from_core)
    direct[0], held = together(direct[0], held)
    counts, = together(token_counts, held)[:1]
    prepared = prepare(0, counts)
    for i, mask in enumerate(reversed(masks)):
        fresh = direct[i : i + 1] + [flip(x, dz=mask) for x in line[1:]]
        if i == levels - 1:
            fresh[-1], *prepared = together(fresh[-1], *prepared)
        if i == 0:
            across = across + [flip(x, dy=1) for x in fresh]
        else:
            across = across + [
                flip(across[k], dz=mask) if k % 2 == 0 else flip(fresh[k], dy=1)
                for k in range(len(fresh))
            ]
        line = line + fresh

    counts = together(token_counts, across[1])[0]
    *prepared, first_weight = prepare(1, counts, gate_up_weight[0], prepared)
    def feed(x):
        gate = x[:, D:].astype(f32)
        picked = (experts == position).astype(f32)
        weight = jnp.sum(
            (gate[:, :peer_count] + gate[:, peer_count : 2 * peer_count]) * picked, axis=1
        )
        gate_up = jnp.dot(x[:, :D], first_weight, preferred_element_type=f32)
        activated = (jax.nn.silu(gate_up[:, :FF]) * gate_up[:, FF:]).astype(bf16)
        produced = jnp.dot(activated, down_weight[0], preferred_element_type=f32)
        return (produced * weight[:, None]).astype(bf16)

    far = jnp.concatenate(across)
    near = jnp.concatenate(line)
    near = feed(together(jnp.concatenate([near, flip(near, ds=1)]), far)[0])
    far = jnp.concatenate([far, flip(far, ds=1)])
    ways = [dict(dy=1)] + [dict(dz=mask) for mask in masks]
    up = []
    for level in range(levels):
        n = held.shape[0] // 2
        came = flip(held[n:], **ways[level])
        if level == 0:
            came, *prepared = together(came, *prepared)
        elif level == 1:
            came = together(came, near)[0]
        up.append((held[:n], came))
        held = choose(3 + 2 * level, held[:n], came)
    needed = flip(held, **ways[levels])
    def chip_sum(fed):
        n = fed.shape[0] // 2
        return fed[:n].astype(f32) + flip(fed[n:], ds=1).astype(f32)

    far = chip_sum(feed(together(far, near)[0])).astype(bf16)
    near = chip_sum(near)
    needed = together(needed, far)[0]

    for level in range(levels - 1, -1, -1):
        own_half, came = up[level]
        back = flip(choose(2 + 2 * level, own_half, needed), **ways[level])
        needed = jnp.concatenate([choose(2 + 2 * level, came, needed), back])
    other = flip(choose(1, keep, needed), ds=1)

    def chunk(x, k):
        return x[k * row_total : (k + 1) * row_total]

    def along(parts):
        for mask in masks[:-1]:
            n = len(parts) // 2
            parts = [
                parts[k].astype(f32) + flip(parts[k + n].astype(bf16), dz=mask).astype(f32)
                for k in range(n)
            ]
        return parts[0].astype(f32)

    arrived = [flip(chunk(far, k), dy=1) for k in range(1, outer, 2)]
    crossed = [chunk(near, k) + arrived[k // 2].astype(f32) for k in range(1, outer, 2)]
    near_sum = along([chunk(near, k) for k in range(0, outer, 2)])
    far_later = together(far, arrived[-1])[0]
    far_sum = along([chunk(far_later, k) for k in range(0, outer, 2)])
    own_sum = near_sum + flip(far_sum.astype(bf16), dy=1).astype(f32)
    mirrored = flip(along(crossed).astype(bf16), dz=masks[-1])

    heads = H

    def head_spec(n, m):
        return pl.BlockSpec((1, heads, n, m), lambda r, g, swaps, at: (r, g, 0, 0))

    resident = pl.BlockSpec(memory_space=pltpu.VMEM)

    def state_index(r, g, swaps, at):
        inside = jnp.bool_(False)
        for p in range(side_count):
            one, two = lax.div(swaps[p, 0], local_reqs), lax.div(swaps[p, 1], local_reqs)
            inside = inside | ((one == at[0]) & (two == at[0]))
        return (jnp.where(inside, local_reqs - 1 - r, r), g, 0, 0)

    new_states, attention_out = pl.pallas_call(
        functools.partial(finish_kernel, heads, block_rows, side_count, levels - 1),
        out_shape=(
            jax.ShapeDtypeStruct(states.shape, f32),
            jax.ShapeDtypeStruct(query_vectors.shape, bf16),
        ),
        grid_spec=pltpu.PrefetchScalarGridSpec(
            num_scalar_prefetch=2,
            grid=(local_reqs, H // heads),
            in_specs=[pl.BlockSpec((1, heads, DK, DV), state_index)] + [resident] * 7,
            out_specs=[
                head_spec(DK, DV),
                pl.BlockSpec((1, T_MAX, heads * DV), lambda r, g, swaps, at: (r, 0, g)),
            ],
        ),
        compiler_params=pltpu.CompilerParams(vmem_limit_bytes=VMEM_LIMIT),
        name="finish",
    )(swap_pairs, here, states, needed, from_core, other, *prepared)
    mirrored = together(mirrored, attention_out)[0]
    expert_out = (own_sum + mirrored.astype(f32)).astype(bf16).reshape(local_reqs, T_MAX, D)
    return (new_states, attention_out, expert_out)


def solution(mesh):
    slots = P(("groups", "dev", "side"))
    experts = P(("dev", "side"))
    in_specs = (slots, P("groups")) + (slots,) * 9 + (experts, experts)
    return jax.shard_map(
        per_device, mesh=mesh, in_specs=in_specs, out_specs=(slots, slots, slots), check_vma=False
    )
```

```python
import functools

import jax
import jax.numpy as jnp
from jax import lax
from jax.experimental import pallas as pl
from jax.experimental.pallas import tpu as pltpu
from jax.sharding import PartitionSpec as P

D = 2304
FF = 512
H = 16
DK = 128
DV = 128
TOP = 8
T_MAX = 16
AXES = ("dev", "side")
HIGHEST = lax.Precision.HIGHEST
VMEM_LIMIT = 16 * 1024 * 1024


def dot_nt(a, b):
    return lax.dot_general(
        a, b, (((1,), (1,)), ((), ())), precision=HIGHEST, preferred_element_type=jnp.float32
    )


def dot_nn(a, b):
    return lax.dot_general(
        a, b, (((1,), (0,)), ((), ())), precision=HIGHEST, preferred_element_type=jnp.float32
    )


def rows_kernel(experts, hidden_ref, ids_ref, gates_ref, out_ref):
    width = out_ref.shape[1] - D
    for r in range(hidden_ref.shape[0]):
        here = slice(r * T_MAX, (r + 1) * T_MAX)
        out_ref[here, :D] = hidden_ref[r]
        number = lax.broadcasted_iota(jnp.int32, (experts, T_MAX), 0)
        table = jnp.zeros((experts, T_MAX), jnp.float32)
        for k in range(TOP):
            table = jnp.where(ids_ref[r, k : k + 1] == number, gates_ref[r, k : k + 1], table)
        high = table.astype(jnp.bfloat16).astype(jnp.float32)
        parts = [high, table - high]
        if width > 2 * experts:
            parts.append(jnp.zeros((width - 2 * experts, T_MAX), jnp.float32))
        out_ref[here, D:] = jnp.transpose(jnp.concatenate(parts, axis=0)).astype(jnp.bfloat16)


def chip_of(position, sides, bits):
    dev = lax.div(position, sides)
    line_at = lax.shift_right_logical(dev, 1)
    gray = jnp.bitwise_xor(line_at, lax.shift_right_logical(line_at, 1))
    chip = jnp.bitwise_and(dev, 1)
    for bit in range(bits):
        chip = chip * 2 + jnp.bitwise_and(lax.shift_right_logical(gray, bit), 1)
    return chip


def pack_kernel(sides, slots, levels, swaps, where_at, send_in, keep_in, send_ref, keep_ref, plan):
    count = send_ref.shape[0]
    swapped = lax.rem(chip_of(where_at[0], sides, levels - 1), count)
    for k in range(count):
        send_ref[k] = send_in[0, jnp.bitwise_xor(swapped, k)].astype(jnp.bfloat16)
        keep_ref[k] = keep_in[0, jnp.bitwise_xor(swapped, k)].astype(jnp.bfloat16)

    @pl.when(pl.program_id(0) == 0)
    def _():
        position = where_at[0]
        pair = lax.rem(position, sides)
        one = lax.div(swaps[pair, 0], slots)
        two = lax.div(swaps[pair, 1], slots)
        me = lax.div(position, sides)
        x = lax.div(one, sides)
        y = lax.div(two, sides)
        flags = [(one == position) | (two == position), (x == me) & (y == me) & (one != two)]
        for level in range(levels):
            near = (x == me) | (y == me)
            differ = x != y
            x, y, me = x >> 1, y >> 1, me >> 1
            flags.extend([differ & (x == me) & (y == me), near])
        row = lax.broadcasted_iota(jnp.int32, plan.shape, 0)
        value = jnp.zeros(plan.shape, jnp.int32)
        for i, flag in enumerate(flags):
            value = jnp.where(row == i, flag.astype(jnp.int32), value)
        plan[...] = value.astype(jnp.float32).astype(plan.dtype)


def unit(vectors):
    return vectors * lax.rsqrt(jnp.sum(vectors * vectors, axis=-1, keepdims=True) + 1e-06)


def fetch_and_prep_kernel(r, counts, weight_ref, *refs):
    fetch = pltpu.make_async_copy(weight_ref, refs[-2], refs[-1])
    fetch.start()
    prep_kernel(r, counts, *refs[:-2])
    fetch.wait()


def prep_kernel(r, counts, q_ref, k_ref, v_ref, decay_ref, rate_ref, *refs):
    z_ref, uo_ref, key_ref, kept_ref = refs[-4:]
    count = counts[r]
    times = lax.broadcasted_iota(jnp.int32, (T_MAX, 1), 0)
    live = (times < count).astype(jnp.float32)
    rows = lax.broadcasted_iota(jnp.int32, (T_MAX, T_MAX), 0)
    cols = lax.broadcasted_iota(jnp.int32, (T_MAX, T_MAX), 1)
    lower = (cols <= rows).astype(jnp.float32)
    decay = decay_ref[0] * live
    total = dot_nn(lower, decay)
    rates = rate_ref[0] * live
    for h in range(q_ref.shape[2] // DK):
        lanes = slice(h * DK, (h + 1) * DK)
        cum = total[:, lanes]
        grown = jnp.exp(-cum)
        key = unit(k_ref[0, :, lanes].astype(jnp.float32))
        query = unit(q_ref[0, :, lanes].astype(jnp.float32)) * live
        value = v_ref[0, :, lanes].astype(jnp.float32)
        rate = rates[:, h : h + 1]
        key_in = key * grown
        query_in = query * grown
        key_out = key * jnp.exp(cum)
        gram = dot_nt(jnp.concatenate([key_in, query_in], axis=0), key_out)
        mix = jnp.where(cols < rows, gram[:T_MAX], 0.0) * rate
        read = jnp.where(cols <= rows, gram[T_MAX:], 0.0)
        solved = jnp.concatenate([value, key_in], axis=1) * rate
        for s in range(T_MAX - 1):
            solved = solved - mix[:, s : s + 1] * solved[s : s + 1, :]
        seen = dot_nn(read, solved)
        high, low = split(jnp.concatenate([solved[:, DV:], query_in - seen[:, DV:]], axis=0))
        z_ref[0, h] = jnp.concatenate([high, low], axis=0)
        uo_ref[0, h, :T_MAX] = solved[:, :DV]
        uo_ref[0, h, T_MAX:] = seen[:, :DV]
        last = cum[T_MAX - 1 : T_MAX]
        high, low = split(key * jnp.exp(cum - last))
        key_ref[0, h] = jnp.concatenate([high, high, low], axis=0)
        kept_ref[0, h] = jnp.broadcast_to(jnp.exp(-last), (8, DK))


def split(x):
    high = x.astype(jnp.bfloat16)
    return high, (x - high.astype(jnp.float32)).astype(jnp.bfloat16)


def finish_kernel(
    heads,
    block_rows,
    sides,
    bits,
    swaps,
    where_at,
    states_ref,
    mine,
    near,
    other,
    z_ref,
    uo_ref,
    key_ref,
    kept_ref,
    new_ref,
    out_ref,
):
    r = pl.program_id(0)
    first = pl.program_id(1) * heads
    position = where_at[0]
    slots = z_ref.shape[0]
    chip = chip_of(position, sides, bits)
    source = jnp.int32(0)
    for p in range(swaps.shape[0]):
        one = lax.div(swaps[p, 0], slots)
        two = lax.div(swaps[p, 1], slots)
        apart = lax.div(one, sides) == lax.div(two, sides)
        kind = jnp.where(lax.rem(position, sides) == p, jnp.where(apart, 3, 2), 4)
        kind = jnp.where(one == two, 1, kind)
        slot = position * slots + r
        source = jnp.where((swaps[p, 0] == slot) | (swaps[p, 1] == slot), kind, source)
    def steps(gathered):
        for h in range(heads):
            row = (first + h) * DK
            block = jnp.bitwise_xor(lax.div(row, block_rows), chip)
            at = pl.ds(pl.multiple_of(lax.rem(row, block_rows), DK), DK)
            state = states_ref[0, h] if gathered is None else gathered[block, at].astype(jnp.float32)
            both = jnp.dot(z_ref[r, first + h], state.astype(jnp.bfloat16), preferred_element_type=jnp.float32)
            both = both[: 2 * T_MAX] + both[2 * T_MAX :]
            writes = uo_ref[r, first + h, :T_MAX] - both[:T_MAX]
            read = uo_ref[r, first + h, T_MAX:] + both[T_MAX:]
            out_ref[0, :, h * DV : (h + 1) * DV] = read.astype(out_ref.dtype)
            high, low = split(writes)
            written = lax.dot_general(
                key_ref[r, first + h],
                jnp.concatenate([high, low, high], axis=0),
                (((0,), (0,)), ((), ())),
                preferred_element_type=jnp.float32,
            )
            new_ref[0, h] = jnp.transpose(kept_ref[r, first + h])[:, :1] * state + written

    for kind, gathered in ((2, mine), (3, near), (4, other)):
        pl.when(source == kind)(functools.partial(steps, gathered))
    pl.when(source < 2)(functools.partial(steps, None))


def per_device(
    states,
    swap_pairs,
    token_counts,
    query_vectors,
    key_vectors,
    value_vectors,
    decay_log,
    write_rate,
    hidden_rows,
    expert_ids,
    route_weights,
    gate_up_weight,
    down_weight,
):
    local_reqs = states.shape[0]
    dev_count = lax.axis_size("dev")
    side_count = lax.axis_size("side")
    peer_count = dev_count * side_count
    position = lax.axis_index(AXES)
    inner = 2
    outer = dev_count // inner
    masks = []
    while len(masks) == 0 or masks[-1] + 1 < outer:
        masks.append(2 ** (len(masks) + 1) - 1)
    f32, bf16 = jnp.float32, jnp.bfloat16

    def flip(x, dz=0, dy=0, ds=0):
        pairs = []
        for d in range(dev_count):
            for s in range(side_count):
                to = (((d // inner) ^ dz) * inner + ((d % inner) ^ dy)) * side_count + (s ^ ds)
                pairs.append((d * side_count + s, to))
        return lax.ppermute(x, AXES, pairs)

    row_total = local_reqs * T_MAX
    experts = jnp.arange(peer_count, dtype=jnp.int32)
    width = D + -(-2 * peer_count // 128) * 128
    row = pl.pallas_call(
        functools.partial(rows_kernel, peer_count),
        out_shape=jax.ShapeDtypeStruct((row_total, width), bf16),
        name="rows",
    )(hidden_rows, jnp.swapaxes(expert_ids, 1, 2), jnp.swapaxes(route_weights, 1, 2))
    def together(*values):
        return lax.optimization_barrier(values)

    line = [row]
    across = [flip(row, dy=1)]
    direct = [flip(row, dz=mask) for mask in reversed(masks)]

    blocks = dev_count // 2
    block_rows = H * DK // blocks
    levels = len(masks)
    here = position.astype(jnp.int32).reshape(1)

    def state_spec(own):
        def index(g, swaps, at):
            pair = lax.rem(at[0], side_count)
            pair = pair if own else 1 - pair
            one, two = swaps[pair, 0], swaps[pair, 1]
            held = jnp.where(lax.div(one, local_reqs) == at[0], one, two)
            return (lax.rem(held, local_reqs), 0, 0, 0)

        return pl.BlockSpec((1, blocks, block_rows, DV), index)

    packed = jax.ShapeDtypeStruct((blocks, block_rows, DV), bf16)
    out_spec = pl.BlockSpec((blocks, block_rows, DV), lambda g, swaps, at: (g, 0, 0))
    state_blocks = states.reshape(local_reqs, blocks, block_rows, DV)
    send, keep, plan = pl.pallas_call(
        functools.partial(pack_kernel, side_count, local_reqs, levels),
        out_shape=(packed, packed, jax.ShapeDtypeStruct((16, DV), bf16)),
        grid_spec=pltpu.PrefetchScalarGridSpec(
            num_scalar_prefetch=2,
            grid=(1,),
            in_specs=[state_spec(False), state_spec(True)],
            out_specs=[out_spec, out_spec, pl.BlockSpec((16, DV), lambda g, swaps, at: (0, 0))],
        ),
        compiler_params=pltpu.CompilerParams(vmem_limit_bytes=VMEM_LIMIT),
        name="pack",
    )(swap_pairs, here, state_blocks, state_blocks)
    from_core = flip(send, ds=1)

    lanes = H * DK
    per_head = [
        (4 * T_MAX, DK, bf16),
        (2 * T_MAX, DV, f32),
        (3 * T_MAX, DK, bf16),
        (8, DK, f32),
    ]

    def prepare(r, counts, weight=None, earlier=()):
        anywhere = [pl.BlockSpec(memory_space=pl.ANY)]
        fetched = [] if weight is None else [weight]
        return pl.pallas_call(
            functools.partial(fetch_and_prep_kernel if fetched else prep_kernel, r),
            out_shape=[jax.ShapeDtypeStruct((local_reqs, H, n, m), t) for n, m, t in per_head]
            + fetched,
            grid_spec=pltpu.PrefetchScalarGridSpec(
                num_scalar_prefetch=1,
                grid=(1,),
                in_specs=anywhere * len(fetched)
                + [pl.BlockSpec((1, T_MAX, lanes), lambda g, c: (r, 0, 0))] * 4
                + [pl.BlockSpec((1, T_MAX, H), lambda g, c: (r, 0, 0))]
                + anywhere * len(earlier),
                out_specs=[
                    pl.BlockSpec((1, H, n, m), lambda g, c: (r, 0, 0, 0)) for n, m, t in per_head
                ]
                + anywhere * len(fetched),
                scratch_shapes=[pltpu.SemaphoreType.DMA] * len(fetched),
            ),
            input_output_aliases={6 + len(fetched) + i: i for i in range(len(earlier))},
            compiler_params=pltpu.CompilerParams(vmem_limit_bytes=VMEM_LIMIT),
            name=f"prep{r}",
        )(
            counts,
            *fetched,
            query_vectors,
            key_vectors,
            value_vectors,
            decay_log,
            write_rate,
            *earlier,
        )

    def choose(flag, yes, no):
        return jnp.where(plan[flag] > 0, yes, no)

    held = choose(0, keep, from_core)
    direct[0], held = together(direct[0], held)
    counts, = together(token_counts, held)[:1]
    prepared = prepare(0, counts)
    for i, mask in enumerate(reversed(masks)):
        fresh = direct[i : i + 1] + [flip(x, dz=mask) for x in line[1:]]
        if i == levels - 1:
            fresh[-1], *prepared = together(fresh[-1], *prepared)
        if i == 0:
            across = across + [flip(x, dy=1) for x in fresh]
        else:
            across = across + [
                flip(across[k], dz=mask) if k % 2 == 0 else flip(fresh[k], dy=1)
                for k in range(len(fresh))
            ]
        line = line + fresh

    counts = together(token_counts, across[1])[0]
    *prepared, first_weight = prepare(1, counts, gate_up_weight[0], prepared)
    def feed(x):
        gate = x[:, D:].astype(f32)
        picked = (experts == position).astype(f32)
        weight = jnp.sum(
            (gate[:, :peer_count] + gate[:, peer_count : 2 * peer_count]) * picked, axis=1
        )
        gate_up = jnp.dot(x[:, :D], first_weight, preferred_element_type=f32)
        activated = (jax.nn.silu(gate_up[:, :FF]) * gate_up[:, FF:]).astype(bf16)
        produced = jnp.dot(activated, down_weight[0], preferred_element_type=f32)
        return (produced * weight[:, None]).astype(bf16)

    far = jnp.concatenate(across)
    near = jnp.concatenate(line)
    near = feed(together(jnp.concatenate([near, flip(near, ds=1)]), far)[0])
    far = jnp.concatenate([far, flip(far, ds=1)])
    ways = [dict(dy=1)] + [dict(dz=mask) for mask in masks]
    up = []
    for level in range(levels):
        n = held.shape[0] // 2
        came = flip(held[n:], **ways[level])
        if level == 0:
            came, *prepared = together(came, *prepared)
        elif level == 1:
            came = together(came, near)[0]
        up.append((held[:n], came))
        held = choose(3 + 2 * level, held[:n], came)
    needed = flip(held, **ways[levels])
    def chip_sum(fed):
        n = fed.shape[0] // 2
        return fed[:n].astype(f32) + flip(fed[n:], ds=1).astype(f32)

    far = chip_sum(feed(together(far, near)[0])).astype(bf16)
    near = chip_sum(near)
    needed = together(needed, far)[0]

    for level in range(levels - 1, -1, -1):
        own_half, came = up[level]
        back = flip(choose(2 + 2 * level, own_half, needed), **ways[level])
        needed = jnp.concatenate([choose(2 + 2 * level, came, needed), back])
    other = flip(choose(1, keep, needed), ds=1)

    def chunk(x, k):
        return x[k * row_total : (k + 1) * row_total]

    def along(parts):
        for mask in masks[:-1]:
            n = len(parts) // 2
            parts = [
                parts[k].astype(f32) + flip(parts[k + n].astype(bf16), dz=mask).astype(f32)
                for k in range(n)
            ]
        return parts[0].astype(f32)

    arrived = [flip(chunk(far, k), dy=1) for k in range(1, outer, 2)]
    crossed = [chunk(near, k) + arrived[k // 2].astype(f32) for k in range(1, outer, 2)]
    near_sum = along([chunk(near, k) for k in range(0, outer, 2)])
    far_later = together(far, arrived[-1])[0]
    far_sum = along([chunk(far_later, k) for k in range(0, outer, 2)])
    own_sum = near_sum + flip(far_sum.astype(bf16), dy=1).astype(f32)
    mirrored = flip(along(crossed).astype(bf16), dz=masks[-1])

    heads = H

    def head_spec(n, m):
        return pl.BlockSpec((1, heads, n, m), lambda r, g, swaps, at: (r, g, 0, 0))

    resident = pl.BlockSpec(memory_space=pltpu.VMEM)

    def state_index(r, g, swaps, at):
        inside = jnp.bool_(False)
        for p in range(side_count):
            one, two = lax.div(swaps[p, 0], local_reqs), lax.div(swaps[p, 1], local_reqs)
            inside = inside | ((one == at[0]) & (two == at[0]))
        return (jnp.where(inside, local_reqs - 1 - r, r), g, 0, 0)

    new_states, attention_out = pl.pallas_call(
        functools.partial(finish_kernel, heads, block_rows, side_count, levels - 1),
        out_shape=(
            jax.ShapeDtypeStruct(states.shape, f32),
            jax.ShapeDtypeStruct(query_vectors.shape, bf16),
        ),
        grid_spec=pltpu.PrefetchScalarGridSpec(
            num_scalar_prefetch=2,
            grid=(local_reqs, H // heads),
            in_specs=[pl.BlockSpec((1, heads, DK, DV), state_index)] + [resident] * 7,
            out_specs=[
                head_spec(DK, DV),
                pl.BlockSpec((1, T_MAX, heads * DV), lambda r, g, swaps, at: (r, 0, g)),
            ],
        ),
        compiler_params=pltpu.CompilerParams(vmem_limit_bytes=VMEM_LIMIT),
        name="finish",
    )(swap_pairs, here, states, needed, from_core, other, *prepared)
    mirrored = together(mirrored, attention_out)[0]
    expert_out = (own_sum + mirrored.astype(f32)).astype(bf16).reshape(local_reqs, T_MAX, D)
    return (new_states, attention_out, expert_out)


def solution(mesh):
    slots = P(("groups", "dev", "side"))
    experts = P(("dev", "side"))
    in_specs = (slots, P("groups")) + (slots,) * 9 + (experts, experts)
    return jax.shard_map(
        per_device, mesh=mesh, in_specs=in_specs, out_specs=(slots, slots, slots), check_vma=False
    )
```
